512 devices in a mesh: dp: 32 (over z_hi, y, core), tensor: 16 (over z_lo, x).
Axes of the slice: x: 4, y: 8, z: 8 (z_hi: 2, z_lo: 4; z = z_hi * 4 + z_lo), core: 2. Of those that a mesh axis runs over, the one named last changes fastest.
Arguments:
- activ: bfloat16 [8192, 4096], P('tensor', 'dp'), may hold values from -6 to 6
- random_sign_flags: int32 [8192], P('tensor'), may hold values from 0 to 1
- codes: int32 [8192, 1024], P('tensor'), may hold values from 0 to 65535
- scales: bfloat16 [64, 4096], P('tensor'), may hold values from 0.0009994507 to 0.0039978027
- adapter_down_map: bfloat16 [8192, 64], P('tensor'), may hold values from -0.0625 to 0.0625
- adapter_up_map: bfloat16 [64, 4096], replicated, may hold values from -0.75 to 0.75
- cotangent: bfloat16 [4096, 4096], P('tensor', 'dp'), may hold values from -6 to 6
Outputs:
- out: bfloat16 [4096, 4096], P('tensor', 'dp')
- input_gradient: bfloat16 [8192, 4096], P('tensor', 'dp')
- down_map_gradient: float32 [8192, 64], P('tensor')
- up_map_gradient: float32 [64, 4096], P(None, 'tensor')
The draws below stay inside these ranges and needn't reach their ends.
Inputs may be any that keep to these rules, and one draw needn't show every extreme that they name: Each word packs the codes of four consecutive output features, the lowest four bits for the first.
All inputs are finite; a program needn't handle non-finite values.
Results may differ from the reference program's by a relative error of at most 0.0055.
Values may be sent and summed in bfloat16 or wider, within the bound.
No kernel may reach another device: no remote copies, remote signals or barrier semaphores. Data moves between devices by JAX's collectives and lax.ppermute only.
A program may use at most 128 MiB of HBM per device.

```python
import math
import jax
import jax.numpy as jnp
from jax import lax

HEADS = 64
INPUT_FEATURES = 8192
OUTPUT_FEATURES = 4096
ADAPTER_RANK = 64
GROUP = 128
TOKEN_ROWS = 4096


def set_ends(array, key, least, largest):
    shape = array.shape
    index_at = [jax.random.randint(jax.random.fold_in(key, axis), (), 0, shape[axis]) for axis in range(len(shape))]
    array = array.at[tuple(index_at)].set(least)
    longest = shape.index(max(shape))
    index_at[longest] = (index_at[longest] + 1) % shape[longest]
    return array.at[tuple(index_at)].set(largest)


def block_scale(stream_key, extent, cuts, low, high):
    level, own = 1.0, jax.random.fold_in(stream_key, 6)
    for position, blocks in cuts:
        draws = jnp.exp(jax.random.uniform(jax.random.fold_in(own, position), (blocks,), jnp.float32, low / len(cuts), high / len(cuts)))
        level = level * jnp.repeat(draws, extent[position] // blocks).reshape([-1 if axis == position else 1 for axis in range(len(extent))])
    return level


def bell_draw(stream_key, shape, deviation, limit, cuts=(), held_as=jnp.bfloat16):
    entries = jax.random.normal(stream_key, shape, jnp.float32) * deviation
    if len(cuts) > 0:
        entries = block_scale(stream_key, shape, cuts, -0.22, 0.18) * entries
    return jnp.clip(entries, min=-limit, max=limit).astype(held_as)


def setup_inputs(seed: int = 0) -> dict:
    seeds = jax.random.split(jax.random.key(seed), 8)
    activ = bell_draw(seeds[0], (INPUT_FEATURES, TOKEN_ROWS), 1.0, 6.0, ((0, 16), (1, 32)))
    random_sign_flags = set_ends(jax.random.randint(seeds[1], (INPUT_FEATURES,), 0, 2), jax.random.fold_in(seeds[1], 1), 0, 1).astype(jnp.int32)
    codes = set_ends(jax.random.randint(seeds[2], (INPUT_FEATURES, OUTPUT_FEATURES // 4), 0, 65536), jax.random.fold_in(seeds[2], 1), 0, 65535).astype(jnp.int32)
    scales = jnp.clip(jnp.exp(math.log(0.0039978027) - 1.3862944 * jax.random.uniform(seeds[3], (INPUT_FEATURES // GROUP, OUTPUT_FEATURES), jnp.float32) ** block_scale(seeds[3], (INPUT_FEATURES // GROUP, OUTPUT_FEATURES), ((0, 16),), -0.2, 0.2)), 0.0009994507, 0.0039978027).astype(jnp.bfloat16)
    adapter_down_map = bell_draw(seeds[4], (INPUT_FEATURES, ADAPTER_RANK), INPUT_FEATURES ** -0.5, 0.0625, ((0, 16),))
    adapter_up_map = bell_draw(seeds[5], (ADAPTER_RANK, OUTPUT_FEATURES), ADAPTER_RANK ** -0.5, 0.75)
    cotangent = bell_draw(seeds[6], (OUTPUT_FEATURES, TOKEN_ROWS), 1.0, 6.0, ((0, 16), (1, 32)))
    return dict(activ=activ, random_sign_flags=random_sign_flags, codes=codes, scales=scales, adapter_down_map=adapter_down_map, adapter_up_map=adapter_up_map, cotangent=cotangent)


ADAPTER_SCALE = 0.5

def hadamard(order):
    counter = jnp.arange(order, dtype=jnp.int32)
    parity = jnp.zeros((order, order), jnp.int32)
    for bit_index in range(order.bit_length() - 1):
        parity = parity + (counter[:, None] >> bit_index & 1) * (counter[None, :] >> bit_index & 1)
    return (1 - 2 * (parity % 2)).astype(jnp.float32)

def dequant(codes, scales):
    offsets = jnp.arange(4, dtype=jnp.int32) * 4
    nibbles = codes[:, :, None] >> offsets & 15
    nibbles = nibbles.reshape(codes.shape[0], codes.shape[1] * 4)
    in_count = nibbles.shape[0]
    output_feature_count = nibbles.shape[1]
    values = (nibbles - 8).astype(jnp.float32).reshape(in_count // GROUP, GROUP, output_feature_count)
    values = values * scales.astype(jnp.float32)[:, None, :]
    return values.reshape(in_count, output_feature_count).astype(jnp.bfloat16)

def reference(activ, random_sign_flags, codes, scales, adapter_down_map, adapter_up_map, cotangent):
    upper_bound = lax.Precision.HIGHEST
    flips = (2 * random_sign_flags - 1).astype(jnp.float32)[:, None]
    table = hadamard(HEADS)
    root = math.sqrt(HEADS)
    signed = (activ.astype(jnp.float32) * flips).reshape(HEADS, -1)
    rotated_input = (jnp.dot(table, signed, precision=upper_bound) / root).reshape(activ.shape).astype(jnp.bfloat16)
    weight = dequant(codes, scales)
    down_product = jnp.dot(adapter_down_map.T, rotated_input, preferred_element_type=jnp.float32)
    up_matrix_wide = adapter_up_map.astype(jnp.float32)
    quantized_product = jnp.dot(weight.T, rotated_input, preferred_element_type=jnp.float32)
    out = (quantized_product + ADAPTER_SCALE * jnp.dot(up_matrix_wide.T, down_product, precision=upper_bound)).astype(jnp.bfloat16)
    reverse_rows = jnp.dot(adapter_up_map, cotangent, preferred_element_type=jnp.float32)
    rotated_gradient = jnp.dot(weight, cotangent, preferred_element_type=jnp.float32)
    rotated_gradient = rotated_gradient + ADAPTER_SCALE * jnp.dot(adapter_down_map.astype(jnp.float32), reverse_rows, precision=upper_bound)
    turned = jnp.dot(table, rotated_gradient.reshape(HEADS, -1), precision=upper_bound).reshape(rotated_gradient.shape)
    input_gradient = (flips * (turned / root)).astype(jnp.bfloat16)
    multiplier = ADAPTER_SCALE / math.sqrt(TOKEN_ROWS)
    down_map_gradient = multiplier * jnp.dot(rotated_input.astype(jnp.float32), reverse_rows.T, precision=upper_bound)
    up_map_gradient = multiplier * jnp.dot(down_product, cotangent.astype(jnp.float32).T, precision=upper_bound)
    return (out, input_gradient, down_map_gradient, up_map_gradient)
```

```python
import jax
import jax.numpy as jnp
from jax import lax
from jax.experimental import pallas as pl
from jax.experimental.pallas import tpu as pltpu
from jax.sharding import PartitionSpec as P

HEADS = 64
GROUP = 128
RANK = 64
NT = 16
F = 512
O = 256
C = 1024
T = 128
ADAPTER_SCALE = 0.5
F32 = jnp.float32
BF16 = jnp.bfloat16
PARAMS = pltpu.CompilerParams(vmem_limit_bytes=40 * 1024 * 1024)
VMEM = pl.BlockSpec(memory_space=pltpu.VMEM)
SMEM = pl.BlockSpec(memory_space=pltpu.SMEM)


def dot(a, b):
    return jnp.dot(a, b, preferred_element_type=F32)


def dot_00(a, b):
    return lax.dot_general(a, b, (((0,), (0,)), ((), ())), preferred_element_type=F32)


def dot_11(a, b):
    return lax.dot_general(a, b, (((1,), (1,)), ((), ())), preferred_element_type=F32)


def split(a):
    high = a.astype(BF16)
    return high, (a - high.astype(F32)).astype(BF16)


def butterfly(v, bits):
    n = v.shape[0]
    rest = v.shape[1:]
    for bit in range(bits):
        w = v.reshape((n >> (bit + 1), 2, 1 << bit) + rest)
        low, high = w[:, 0], w[:, 1]
        v = jnp.stack([low + high, low - high], axis=1).reshape((n,) + rest)
    return v


def iota2(shape, dim):
    return lax.broadcasted_iota(jnp.int32, shape, dim)


def weights_kernel(codes, scales, up, weight, up_apart, scales_apart):
    group = pl.program_id(0)

    @pl.when(group == 0)
    def _():
        row, col = iota2((512, 512), 0), iota2((512, 512), 1)
        apart = jnp.where(row == 4 * (col & 127) + (col >> 7), 1.0, 0.0).astype(BF16)
        for block in range(8):
            lanes = slice(512 * block, 512 * (block + 1))
            s = dot(scales[:, lanes], apart)
            u = dot(up[:, lanes], apart).astype(BF16)
            for k in range(4):
                to = slice(128 * block, 128 * (block + 1))
                scales_apart[k, :, to] = s[:, 128 * k : 128 * (k + 1)]
                up_apart[k, :, to] = u[:, 128 * k : 128 * (k + 1)]

    for k in range(4):
        nibble = ((codes[...] >> (4 * k)) & 15) - 8
        scale = scales_apart[k, pl.ds(group, 1), :]
        weight[k] = (nibble.astype(F32) * scale).astype(BF16)


def make_weights(codes, scales, up):
    return pl.pallas_call(
        weights_kernel,
        grid=(F // GROUP,),
        in_specs=[
            pl.BlockSpec((GROUP, C), lambda g: (g, 0)),
            pl.BlockSpec((F // GROUP, 4 * C), lambda g: (0, 0)),
            pl.BlockSpec((RANK, 4 * C), lambda g: (0, 0)),
        ],
        out_specs=[
            pl.BlockSpec((4, GROUP, C), lambda g: (0, g, 0)),
            pl.BlockSpec((4, RANK, C), lambda g: (0, 0, 0)),
        ],
        out_shape=[
            jax.ShapeDtypeStruct((4, F, C), BF16),
            jax.ShapeDtypeStruct((4, RANK, C), BF16),
        ],
        scratch_shapes=[pltpu.VMEM((4, F // GROUP, C), F32)],
        compiler_params=PARAMS,
        cost_estimate=pl.CostEstimate(flops=20_000_000, bytes_accessed=7_000_000, transcendentals=0),
        name="weights",
    )(codes, scales, up)


def pack_kernel(activ, flags, down_map, cot, sent, cot_apart):
    eye = iota2((GROUP, GROUP), 0) == iota2((GROUP, GROUP), 1)
    parts = []
    for h in range(4):
        sign = (2 * flags[h : h + 1, :] - 1).astype(F32)
        diagonal = jnp.where(eye, sign, 0.0).astype(BF16)
        parts.append(dot(diagonal, activ[GROUP * h : GROUP * (h + 1), :]).reshape(NT, 8, T))
    lane, rank = iota2((RANK, 2 * RANK), 1), iota2((RANK, 2 * RANK), 0)
    left = jnp.where(lane == rank, 1.0, 0.0).astype(BF16)
    right = jnp.where(lane == rank + RANK, 1.0, 0.0).astype(BF16)
    for h in (0, 2):
        even = down_map[GROUP * h : GROUP * (h + 1), :]
        odd = down_map[GROUP * (h + 1) : GROUP * (h + 2), :]
        parts.append((dot(even, left) + dot(odd, right)).reshape(NT, 8, T))
    sent[...] = jnp.concatenate(parts, axis=1).astype(BF16)
    row, col = iota2((O, O), 0), iota2((O, O), 1)
    apart = jnp.where(col == 4 * (row & 63) + (row >> 6), 1.0, 0.0).astype(BF16)
    cot_apart[...] = dot(apart, cot[...]).astype(BF16)


def pack(activ, flags, down_map, cot):
    return pl.pallas_call(
        pack_kernel,
        in_specs=[VMEM] * 4,
        out_specs=[VMEM] * 2,
        out_shape=[
            jax.ShapeDtypeStruct((NT, 48, T), BF16),
            jax.ShapeDtypeStruct((O, T), BF16),
        ],
        compiler_params=PARAMS,
        cost_estimate=pl.CostEstimate(flops=60_000_000, bytes_accessed=600_000, transcendentals=0),
        name="pack",
    )(activ, flags, down_map, cot)


def mix_kernel(got, sent):
    v = got[:, 0:32, :].astype(F32).reshape(HEADS, 8, T)
    v = butterfly(v, 6) * 0.125
    mixed = v.reshape(NT, 32, T).astype(BF16)
    sent[:, 0:32, :] = mixed
    pairs = v.reshape(NT, 2, 2, 8, T)
    even = pairs[:, :, 0].reshape(256, T).astype(BF16)
    odd = pairs[:, :, 1].reshape(256, T).astype(BF16)
    maps = got[:, 32:48, :].reshape(256, 2 * RANK)
    down = dot_00(maps, even)[0:RANK] + dot_00(maps, odd)[RANK : 2 * RANK]
    sent[:, 32:96, :] = jnp.broadcast_to(down.astype(BF16)[None], (NT, RANK, T))


def mix(got):
    return pl.pallas_call(
        mix_kernel,
        in_specs=[VMEM],
        out_specs=VMEM,
        out_shape=jax.ShapeDtypeStruct((NT, 96, T), BF16),
        compiler_params=PARAMS,
        cost_estimate=pl.CostEstimate(flops=20_000_000, bytes_accessed=600_000, transcendentals=0),
        name="mix",
    )(got)


def project_kernel(got, weight, cot, shares, mixed, down, up_gradient):
    @pl.when(pl.program_id(0) == 0)
    def _():
        v = got[:, 0:32, :].astype(F32).reshape(NT, 4, 8, T)
        for h in range(4):
            mixed[GROUP * h : GROUP * (h + 1), :] = v[:, h].reshape(GROUP, T).astype(BF16)
        total = jnp.sum(got[:, 32:96, :].astype(F32), axis=0)
        down[...] = total
        high, low = split(total)
        for half in range(2):
            c = cot[GROUP * half : GROUP * (half + 1), :]
            up_gradient[RANK * half : RANK * (half + 1), :] = dot_11(high, c) + dot_11(low, c)

    share = dot_00(weight[0], mixed[...])
    shares[...] = share.reshape(NT, 64, T).astype(BF16)


def project(got, weight, cot):
    return pl.pallas_call(
        project_kernel,
        grid=(4,),
        in_specs=[
            pl.BlockSpec((NT, 96, T), lambda k: (0, 0, 0)),
            pl.BlockSpec((1, F, C), lambda k: (k, 0, 0)),
            pl.BlockSpec((O, T), lambda k: (0, 0)),
        ],
        out_specs=[
            pl.BlockSpec((NT, 64, T), lambda k: (0, k, 0)),
            pl.BlockSpec((F, T), lambda k: (0, 0)),
            pl.BlockSpec((RANK, T), lambda k: (0, 0)),
            pl.BlockSpec((2 * RANK, T), lambda k: (0, 0)),
        ],
        out_shape=[
            jax.ShapeDtypeStruct((NT, O, T), BF16),
            jax.ShapeDtypeStruct((F, T), BF16),
            jax.ShapeDtypeStruct((RANK, T), F32),
            jax.ShapeDtypeStruct((2 * RANK, T), F32),
        ],
        compiler_params=PARAMS,
        cost_estimate=pl.CostEstimate(flops=540_000_000, bytes_accessed=6_000_000, transcendentals=0),
        name="project",
    )(got, weight, cot)


def back_kernel(
    place, own, by1, by2, by3, weight, up_apart, down_map, mixed, up_gradient,
    current, narrow, keep, give, cot, total, back, sums,
):
    k = pl.program_id(0)

    @pl.when(k == 0)
    def _():
        for x, blocks in enumerate((own, by1, by2, by3)):
            for z in range(4):
                source = place[0] ^ (x + 4 * z)
                rows = pl.ds(pl.multiple_of(source * 64, 64), 64)
                for n in range(4):
                    cot[n, rows, :] = blocks[z, 64 * n : 64 * (n + 1), :]
        total[...] = jnp.zeros_like(total)
        back[...] = jnp.zeros_like(back)

    total[...] += dot(weight[0], cot[k])
    back[...] += dot(up_apart[0], cot[k])

    @pl.when(k == 3)
    def _():
        high, low = split(back[...])
        maps = down_map[...]
        g = total[...] + ADAPTER_SCALE * (dot(maps, high) + dot(maps, low))
        g = butterfly(g.reshape(4, GROUP, T), 2).reshape(F, T)
        current[...] = g
        narrow[...] = g.astype(BF16)
        zero = jnp.zeros((RANK, T), BF16)
        for half in range(2):
            m = mixed[256 * half : 256 * (half + 1), :]
            for n, part in enumerate((high, low)):
                side = jnp.concatenate([zero, part] if half else [part, zero], axis=0)
                product = dot_11(m, side)
                if half == 0 and n == 0:
                    gradient = product
                else:
                    gradient = gradient + product
        sums[0:256, :] = gradient
        sums[256:384, :] = up_gradient[...]
        keep[...] = sums[pl.ds(pl.multiple_of(place[1] * 192, 192), 192), :]
        give[...] = sums[pl.ds(pl.multiple_of(192 - place[1] * 192, 192), 192), :]


def backward(place, own, by1, by2, by3, weight, up_apart, down_map, mixed, up_gradient):
    whole2 = lambda k: (0, 0)
    whole3 = lambda k: (0, 0, 0)
    return pl.pallas_call(
        back_kernel,
        grid=(4,),
        in_specs=[SMEM]
        + [pl.BlockSpec((4, O, T), whole3)] * 4
        + [
            pl.BlockSpec((1, F, C), lambda k: (k, 0, 0)),
            pl.BlockSpec((1, RANK, C), lambda k: (k, 0, 0)),
            pl.BlockSpec((F, RANK), whole2),
            pl.BlockSpec((F, T), whole2),
            pl.BlockSpec((2 * RANK, T), whole2),
        ],
        out_specs=[
            pl.BlockSpec((F, T), whole2),
            pl.BlockSpec((F, T), whole2),
            pl.BlockSpec((192, T), whole2),
            pl.BlockSpec((192, T), whole2),
        ],
        out_shape=[
            jax.ShapeDtypeStruct((F, T), F32),
            jax.ShapeDtypeStruct((F, T), BF16),
            jax.ShapeDtypeStruct((192, T), F32),
            jax.ShapeDtypeStruct((192, T), F32),
        ],
        scratch_shapes=[
            pltpu.VMEM((4, C, T), BF16),
            pltpu.VMEM((F, T), F32),
            pltpu.VMEM((RANK, T), F32),
            pltpu.VMEM((384, T), F32),
        ],
        compiler_params=PARAMS,
        cost_estimate=pl.CostEstimate(flops=600_000_000, bytes_accessed=7_000_000, transcendentals=0),
        name="backward",
    )(place, own, by1, by2, by3, weight, up_apart, down_map, mixed, up_gradient)


def finish_kernel(place, shares, up, down, out):
    total = jnp.sum(shares[...].astype(F32), axis=0)
    row, col = iota2((O, O), 0), iota2((O, O), 1)
    together = jnp.where(row == 4 * (col & 63) + (col >> 6), 1.0, 0.0).astype(BF16)
    high, low = split(total)
    own = up[:, pl.ds(pl.multiple_of(place[0] * O, O), O)]
    down_high, down_low = split(down[...])
    adapter = dot_00(own, down_high) + dot_00(own, down_low)
    out[...] = (dot(together, high) + dot(together, low) + ADAPTER_SCALE * adapter).astype(BF16)


def finish(place, shares, up, down):
    return pl.pallas_call(
        finish_kernel,
        in_specs=[SMEM, VMEM, VMEM, VMEM],
        out_specs=VMEM,
        out_shape=jax.ShapeDtypeStruct((O, T), BF16),
        compiler_params=PARAMS,
        cost_estimate=pl.CostEstimate(flops=40_000_000, bytes_accessed=1_700_000, transcendentals=0),
        name="finish",
    )(place, shares, up, down)


def gradients_kernel(place, keep, other, down_gradient, up_gradient, sums):
    multiplier = ADAPTER_SCALE / 64.0
    sums[pl.ds(pl.multiple_of(place[1] * 192, 192), 192), :] = keep[...] * multiplier
    sums[pl.ds(pl.multiple_of(192 - place[1] * 192, 192), 192), :] = other[...] * multiplier
    down_gradient[0:256, :] = sums[0:256, 0:RANK]
    down_gradient[256:512, :] = sums[0:256, RANK : 2 * RANK]
    up_gradient[:, 0:128] = sums[256:320, :]
    up_gradient[:, 128:256] = sums[320:384, :]


def gradients(place, keep, other):
    return pl.pallas_call(
        gradients_kernel,
        in_specs=[SMEM, VMEM, VMEM],
        out_specs=[VMEM, VMEM],
        out_shape=[
            jax.ShapeDtypeStruct((F, RANK), F32),
            jax.ShapeDtypeStruct((RANK, O), F32),
        ],
        scratch_shapes=[pltpu.VMEM((384, T), F32)],
        compiler_params=PARAMS,
        cost_estimate=pl.CostEstimate(flops=100_000, bytes_accessed=500_000, transcendentals=0),
        name="gradients",
    )(place, keep, other)


def by(value, axis, mask):
    pairs = [(source, source ^ mask) for source in range(lax.axis_size(axis))]
    return lax.ppermute(value, axis, pairs)


def local(activ, flags, codes, scales, down_map, up, cot):
    me = lax.axis_index("tensor")
    replica = lax.axis_index("dp")
    place = jnp.stack([me, replica & 1]).astype(jnp.int32)
    sent, cot_apart = pack(activ, flags.reshape(4, GROUP), down_map, cot)
    got = lax.all_to_all(sent, "tensor", 0, 0, tiled=True)
    weight, up_apart = make_weights(codes, scales, up)

    along_z = [cot_apart] + [by(cot_apart, "tensor", 4 * z) for z in (1, 2, 3)]
    own = jnp.stack(along_z)
    by1, by2, by3 = (by(own, "tensor", x) for x in (1, 2, 3))

    got = lax.all_to_all(mix(got), "tensor", 0, 0, tiled=True)
    shares, mixed, down, up_part = project(got, weight, cot)
    shares = lax.all_to_all(shares, "tensor", 0, 0, tiled=True)

    current, narrow, keep, give = backward(
        place, own, by1, by2, by3, weight, up_apart, down_map, mixed, up_part
    )
    keep = keep + by(give, "dp", 1)
    for mask in (2, 4, 8, 16):
        keep = keep + by(keep, "dp", mask)
    down_gradient, up_gradient = gradients(place, keep, by(keep, "dp", 1))

    for bit in range(4):
        partner = by(narrow, "tensor", 1 << bit).astype(F32)
        current = jnp.where((me >> bit) & 1 == 1, partner - current, current + partner)
        narrow = current.astype(BF16)
    sign = (2 * flags - 1).astype(F32)[:, None]
    input_gradient = (sign * (current * 0.125)).astype(BF16)

    out = finish(place, shares, up, down)
    return out, input_gradient, down_gradient, up_gradient


def solution(mesh):
    in_specs = (
        P("tensor", "dp"),
        P("tensor"),
        P("tensor", None),
        P("tensor", None),
        P("tensor", None),
        P(),
        P("tensor", "dp"),
    )
    out_specs = (P("tensor", "dp"), P("tensor", "dp"), P("tensor", None), P(None, "tensor"))
    return jax.shard_map(local, mesh=mesh, in_specs=in_specs, out_specs=out_specs, check_vma=False)
```

```python
import jax
import jax.numpy as jnp
from jax import lax
from jax.experimental import pallas as pl
from jax.experimental.pallas import tpu as pltpu
from jax.sharding import PartitionSpec as P

HEADS = 64
GROUP = 128
RANK = 64
NT = 16
F = 512
O = 256
C = 1024
T = 128
ADAPTER_SCALE = 0.5
F32 = jnp.float32
BF16 = jnp.bfloat16
PARAMS = pltpu.CompilerParams(vmem_limit_bytes=24 * 1024 * 1024)
VMEM = pl.BlockSpec(memory_space=pltpu.VMEM)
SMEM = pl.BlockSpec(memory_space=pltpu.SMEM)
HBM = pl.BlockSpec(memory_space=pltpu.HBM)
DMA = pltpu.SemaphoreType.DMA


def in_hbm(*arrays):
    return [pltpu.with_memory_space_constraint(a, pltpu.HBM) for a in arrays]


def dot(a, b):
    return jnp.dot(a, b, preferred_element_type=F32)


def dot_00(a, b):
    return lax.dot_general(a, b, (((0,), (0,)), ((), ())), preferred_element_type=F32)


def dot_11(a, b):
    return lax.dot_general(a, b, (((1,), (1,)), ((), ())), preferred_element_type=F32)


def split(a):
    high = a.astype(BF16)
    return high, (a - high.astype(F32)).astype(BF16)


def butterfly(v, bits):
    n = v.shape[0]
    rest = v.shape[1:]
    for bit in range(bits):
        w = v.reshape((n >> (bit + 1), 2, 1 << bit) + rest)
        low, high = w[:, 0], w[:, 1]
        v = jnp.stack([low + high, low - high], axis=1).reshape((n,) + rest)
    return v


def iota2(shape, dim):
    return lax.broadcasted_iota(jnp.int32, shape, dim)


def weights_kernel(
    codes_hbm, scales_hbm, up_hbm, weight_out, weight_t_out, up_out,
    codes, scales, up, scales_apart, weight, weight_t, up_apart, sems, out_sems,
):
    copy_scales = pltpu.make_async_copy(scales_hbm, scales, sems.at[4])
    copy_up = pltpu.make_async_copy(up_hbm, up, sems.at[5])
    copies = []
    for g in range(4):
        rows = slice(GROUP * g, GROUP * (g + 1))
        copies.append(pltpu.make_async_copy(codes_hbm.at[rows], codes.at[rows], sems.at[g]))
    copy_scales.start()
    copy_up.start()
    for copy in copies:
        copy.start()
    row, col = iota2((512, 512), 0), iota2((512, 512), 1)
    apart = jnp.where(row == 4 * (col & 127) + (col >> 7), 1.0, 0.0).astype(BF16)
    copy_scales.wait()
    copy_up.wait()
    for block in range(8):
        lanes = slice(512 * block, 512 * (block + 1))
        s = dot(scales[:, lanes], apart)
        u = dot(up[:, lanes], apart).astype(BF16)
        for k in range(4):
            to = slice(128 * block, 128 * (block + 1))
            scales_apart[k, :, to] = s[:, 128 * k : 128 * (k + 1)]
            up_apart[k, :, to] = u[:, 128 * k : 128 * (k + 1)]
    sends = [pltpu.make_async_copy(up_apart, up_out, out_sems.at[5])]
    sends[0].start()
    for g in range(4):
        copies[g].wait()
        rows = slice(GROUP * g, GROUP * (g + 1))
        for k in range(4):
            nibble = ((codes[rows, :] >> (4 * k)) & 15) - 8
            part = nibble.astype(F32) * scales_apart[k, g : g + 1, :]
            weight[k, rows, :] = part.astype(BF16)
            weight_t[k, :, rows] = part.T.astype(BF16)
        sends.append(
            pltpu.make_async_copy(weight.at[:, rows], weight_out.at[:, rows], out_sems.at[g])
        )
        sends[g + 1].start()
    sends.append(pltpu.make_async_copy(weight_t, weight_t_out, out_sems.at[4]))
    sends[5].start()
    for send in sends:
        send.wait()


def make_weights(codes, scales, up):
    return pl.pallas_call(
        weights_kernel,
        in_specs=[HBM] * 3,
        out_specs=[HBM] * 3,
        out_shape=[
            pltpu.HBM((4, F, C), BF16),
            pltpu.HBM((4, C, F), BF16),
            pltpu.HBM((4, RANK, C), BF16),
        ],
        scratch_shapes=[
            pltpu.VMEM((F, C), jnp.int32),
            pltpu.VMEM((F // GROUP, 4 * C), BF16),
            pltpu.VMEM((RANK, 4 * C), BF16),
            pltpu.VMEM((4, F // GROUP, C), F32),
            pltpu.VMEM((4, F, C), BF16),
            pltpu.VMEM((4, C, F), BF16),
            pltpu.VMEM((4, RANK, C), BF16),
            DMA((6,)),
            DMA((6,)),
        ],
        compiler_params=PARAMS,
        cost_estimate=pl.CostEstimate(flops=20_000_000, bytes_accessed=20_000_000, transcendentals=0),
        name="weights",
    )(*in_hbm(codes, scales, up))


def pack_kernel(
    activ_hbm, flags_hbm, down_hbm, cot_hbm, sent,
    activ, flags, down_map, cot, first, own, sems, out_sems,
):
    pairs = ((activ_hbm, activ), (flags_hbm, flags), (down_hbm, down_map), (cot_hbm, cot))
    copies = [pltpu.make_async_copy(a, b, sems.at[n]) for n, (a, b) in enumerate(pairs)]
    for copy in copies:
        copy.start()
    row, col = iota2((O, O), 0), iota2((O, O), 1)
    apart = jnp.where(col == 4 * (row & 63) + (row >> 6), 1.0, 0.0).astype(BF16)
    eye = iota2((GROUP, GROUP), 0) == iota2((GROUP, GROUP), 1)
    lane, rank = iota2((RANK, 2 * RANK), 1), iota2((RANK, 2 * RANK), 0)
    left = jnp.where(lane == rank, 1.0, 0.0).astype(BF16)
    right = jnp.where(lane == rank + RANK, 1.0, 0.0).astype(BF16)
    copies[3].wait()
    own[...] = dot(apart, cot[...]).astype(BF16)
    sends = []
    for q in range(NT):
        sends.append(pltpu.make_async_copy(own, sent.at[q, 48:304], out_sems.at[q]))
        sends[q].start()
    for copy in copies[:3]:
        copy.wait()
    parts = []
    for h in range(4):
        sign = (2 * flags[h : h + 1, :] - 1).astype(F32)
        diagonal = jnp.where(eye, sign, 0.0).astype(BF16)
        parts.append(dot(diagonal, activ[GROUP * h : GROUP * (h + 1), :]).reshape(NT, 8, T))
    for h in (0, 2):
        even = down_map[:, GROUP * h : GROUP * (h + 1)]
        odd = down_map[:, GROUP * (h + 1) : GROUP * (h + 2)]
        parts.append((dot_00(even, left) + dot_00(odd, right)).reshape(NT, 8, T))
    first[...] = jnp.concatenate(parts, axis=1).astype(BF16)
    sends.append(pltpu.make_async_copy(first, sent.at[:, 0:48], out_sems.at[NT]))
    sends[NT].start()
    for send in sends:
        send.wait()


def pack(activ, flags, down_t, cot):
    return pl.pallas_call(
        pack_kernel,
        in_specs=[HBM] * 4,
        out_specs=HBM,
        out_shape=pltpu.HBM((NT, 304, T), BF16),
        scratch_shapes=[
            pltpu.VMEM((F, T), BF16),
            pltpu.VMEM((4, GROUP), jnp.int32),
            pltpu.VMEM((RANK, F), BF16),
            pltpu.VMEM((O, T), BF16),
            pltpu.VMEM((NT, 48, T), BF16),
            pltpu.VMEM((O, T), BF16),
            DMA((4,)),
            DMA((NT + 1,)),
        ],
        compiler_params=PARAMS,
        cost_estimate=pl.CostEstimate(flops=60_000_000, bytes_accessed=2_000_000, transcendentals=0),
        name="pack",
    )(*in_hbm(activ, flags, down_t, cot))


def turn_kernel(
    got, weight_hbm, up_hbm, down_hbm, sent, back_out, cot, weight, up_apart, down_t, sems
):
    copy_up = pltpu.make_async_copy(up_hbm, up_apart, sems.at[4])
    copy_down = pltpu.make_async_copy(down_hbm, down_t, sems.at[5])
    copies = []
    for h in range(4):
        rows = slice(GROUP * h, GROUP * (h + 1))
        copies.append(
            pltpu.make_async_copy(weight_hbm.at[:, rows], weight.at[:, rows], sems.at[h])
        )
    copy_up.start()
    copy_down.start()
    for copy in copies:
        copy.start()
    v = got[:, 0:32, :].astype(F32).reshape(HEADS, 8, T)
    v = butterfly(v, 6) * 0.125
    sent[:, 0:32, :] = v.reshape(NT, 32, T).astype(BF16)
    pairs = v.reshape(NT, 2, 2, 8, T)
    even = pairs[:, :, 0].reshape(256, T).astype(BF16)
    odd = pairs[:, :, 1].reshape(256, T).astype(BF16)
    maps = got[:, 32:48, :].reshape(256, 2 * RANK)
    down = dot_00(maps, even)[0:RANK] + dot_00(maps, odd)[RANK : 2 * RANK]
    down = down.astype(BF16)
    for q in range(NT):
        sent[q, 64:128, :] = down
        for k in range(4):
            cot[k, 64 * q : 64 * (q + 1), :] = got[q, 48 + 64 * k : 112 + 64 * k, :]
    copy_up.wait()
    copy_down.wait()
    back = jnp.zeros((RANK, T), F32)
    for k in range(4):
        back = back + dot(up_apart[k], cot[k])
    back_out[...] = back
    high, low = split(back)
    for h in range(4):
        rows = slice(GROUP * h, GROUP * (h + 1))
        copies[h].wait()
        maps = down_t[:, rows]
        g = ADAPTER_SCALE * (dot_00(maps, high) + dot_00(maps, low))
        for k in range(4):
            g = g + dot(weight[k, rows, :], cot[k])
        cot_rows = g.reshape(NT, 8, T)
        if h % 2 == 0:
            first = cot_rows
        else:
            both = jnp.concatenate([first, cot_rows], axis=1)
            sent[:, 24 + 8 * h : 40 + 8 * h, :] = both.astype(BF16)


def turn(got, weight, up_apart, down_t):
    return pl.pallas_call(
        turn_kernel,
        in_specs=[VMEM] + [HBM] * 3,
        out_specs=[VMEM] * 2,
        out_shape=[
            jax.ShapeDtypeStruct((NT, 128, T), BF16),
            jax.ShapeDtypeStruct((RANK, T), F32),
        ],
        scratch_shapes=[
            pltpu.VMEM((4, C, T), BF16),
            pltpu.VMEM((4, F, C), BF16),
            pltpu.VMEM((4, RANK, C), BF16),
            pltpu.VMEM((RANK, F), BF16),
            DMA((6,)),
        ],
        compiler_params=PARAMS,
        cost_estimate=pl.CostEstimate(flops=600_000_000, bytes_accessed=7_000_000, transcendentals=0),
        name="turn",
    )(got, *in_hbm(weight, up_apart, down_t))


def project_kernel(
    got, weight_hbm, back, cot, sent, down, sums, mixed, weight_t, sems
):
    copies = [pltpu.make_async_copy(weight_hbm.at[k], weight_t.at[k], sems.at[k]) for k in range(4)]
    for copy in copies:
        copy.start()
    v = got[:, 0:32, :].astype(F32).reshape(NT, 4, 8, T)
    for h in range(4):
        mixed[GROUP * h : GROUP * (h + 1), :] = v[:, h].reshape(GROUP, T).astype(BF16)
    g = got[:, 32:64, :].astype(F32).reshape(HEADS, 8, T)
    g = butterfly(g, 6) * 0.125
    sent[:, 256:288, :] = g.reshape(NT, 32, T).astype(BF16)
    total = jnp.sum(got[:, 64:128, :].astype(F32), axis=0)
    down[...] = total
    high, low = split(total)
    back_high, back_low = split(back[...])
    for h in range(4):
        rows = slice(GROUP * h, GROUP * (h + 1))
        product = dot_11(back_high, mixed[rows, :]) + dot_11(back_low, mixed[rows, :])
        sums[RANK * h : RANK * (h + 1), :] = product
    for half in range(2):
        c = cot[GROUP * half : GROUP * (half + 1), :]
        sums[256 + RANK * half : 320 + RANK * half, :] = dot_11(high, c) + dot_11(low, c)
    for k in range(4):
        copies[k].wait()
        share = dot(weight_t[k], mixed[...])
        sent[:, 64 * k : 64 * (k + 1), :] = share.reshape(NT, 64, T).astype(BF16)


def project(got, weight_t, back, cot):
    return pl.pallas_call(
        project_kernel,
        in_specs=[VMEM, HBM, VMEM, VMEM],
        out_specs=[VMEM] * 3,
        out_shape=[
            jax.ShapeDtypeStruct((NT, 288, T), BF16),
            jax.ShapeDtypeStruct((RANK, T), F32),
            jax.ShapeDtypeStruct((384, T), F32),
        ],
        scratch_shapes=[
            pltpu.VMEM((F, T), BF16),
            pltpu.VMEM((4, C, F), BF16),
            DMA((4,)),
        ],
        compiler_params=PARAMS,
        cost_estimate=pl.CostEstimate(flops=540_000_000, bytes_accessed=6_000_000, transcendentals=0),
        name="project",
    )(got, *in_hbm(weight_t), back, cot)


def finish_kernel(place, got, up, down, flags, out, input_gradient, own, sem):
    lanes = pl.ds(pl.multiple_of(place[0] * O, O), O)
    copy = pltpu.make_async_copy(up.at[:, lanes], own, sem)
    copy.start()
    total = jnp.sum(got[:, 0:256, :].astype(F32), axis=0)
    row, col = iota2((O, O), 0), iota2((O, O), 1)
    together = jnp.where(row == 4 * (col & 63) + (col >> 6), 1.0, 0.0).astype(BF16)
    high, low = split(total)
    down_high, down_low = split(down[...])
    copy.wait()
    adapter = dot_00(own[...], down_high) + dot_00(own[...], down_low)
    out[...] = (dot(together, high) + dot(together, low) + ADAPTER_SCALE * adapter).astype(BF16)
    eye = iota2((GROUP, GROUP), 0) == iota2((GROUP, GROUP), 1)
    g = got[:, 256:288, :].astype(F32).reshape(NT, 4, 8, T)
    for h in range(4):
        sign = (2 * flags[h : h + 1, :] - 1).astype(F32)
        diagonal = jnp.where(eye, sign, 0.0).astype(BF16)
        part = g[:, h].reshape(GROUP, T).astype(BF16)
        input_gradient[GROUP * h : GROUP * (h + 1), :] = dot(diagonal, part).astype(BF16)


def finish(place, got, up, down, flags):
    return pl.pallas_call(
        finish_kernel,
        in_specs=[SMEM, VMEM, HBM, VMEM, VMEM],
        out_specs=[VMEM] * 2,
        out_shape=[
            jax.ShapeDtypeStruct((O, T), BF16),
            jax.ShapeDtypeStruct((F, T), BF16),
        ],
        scratch_shapes=[pltpu.VMEM((RANK, O), BF16), DMA(())],
        compiler_params=PARAMS,
        cost_estimate=pl.CostEstimate(flops=40_000_000, bytes_accessed=1_700_000, transcendentals=0),
        name="finish",
    )(place, got, *in_hbm(up), down, flags)


def gradients_kernel(sums, down_gradient, up_gradient):
    multiplier = ADAPTER_SCALE / 64.0
    for h in range(4):
        lanes = slice(GROUP * h, GROUP * (h + 1))
        down_gradient[:, lanes] = sums[RANK * h : RANK * (h + 1), :] * multiplier
    for half in range(2):
        lanes = slice(GROUP * half, GROUP * (half + 1))
        up_gradient[:, lanes] = sums[256 + RANK * half : 320 + RANK * half, :] * multiplier


def gradients(sums):
    return pl.pallas_call(
        gradients_kernel,
        in_specs=[VMEM],
        out_specs=[VMEM, VMEM],
        out_shape=[
            jax.ShapeDtypeStruct((RANK, F), F32),
            jax.ShapeDtypeStruct((RANK, O), F32),
        ],
        compiler_params=PARAMS,
        cost_estimate=pl.CostEstimate(flops=100_000, bytes_accessed=500_000, transcendentals=0),
        name="gradients",
    )(sums)


def by(value, axis, mask):
    pairs = [(source, source ^ mask) for source in range(lax.axis_size(axis))]
    return lax.ppermute(value, axis, pairs)


def exchange(value):
    return lax.all_to_all(value, "tensor", 0, 0, tiled=True)


def both_cores(value):
    groups = [[device, device + 1] for device in range(0, lax.axis_size("dp"), 2)]
    return lax.all_gather(value, "dp", axis=0, tiled=True, axis_index_groups=groups)


def add_partner(value, mask):
    value = value.astype(BF16)
    return value.astype(F32) + by(value, "dp", mask).astype(F32)


def local(activ, flags, codes, scales, down_map, up, cot):
    core = lax.axis_index("dp") & 1
    place = jnp.stack([lax.axis_index("tensor")]).astype(jnp.int32)
    flags = flags.reshape(4, GROUP)
    down_t = down_map.T
    got = exchange(pack(activ, flags, down_t, cot))
    weight, weight_t, up_apart = make_weights(codes, scales, up)
    sent, back = turn(got, weight, up_apart, down_t)
    sent, down, sums = project(exchange(sent), weight_t, back, cot)
    got = exchange(sent)
    two = both_cores(sums)
    half = lax.dynamic_slice_in_dim(two[:384] + two[384:], core * 192, 192)
    for mask in (2, 4, 12, 16):
        half = add_partner(half, mask)
    out, input_gradient = finish(place, got, up, down, flags)
    half, out, input_gradient = lax.optimization_barrier((half, out, input_gradient))
    down_gradient, up_gradient = gradients(both_cores(half))
    return out, input_gradient, down_gradient.T, up_gradient


def solution(mesh):
    in_specs = (
        P("tensor", "dp"),
        P("tensor"),
        P("tensor", None),
        P("tensor", None),
        P("tensor", None),
        P(),
        P("tensor", "dp"),
    )
    out_specs = (P("tensor", "dp"), P("tensor", "dp"), P("tensor", None), P(None, "tensor"))
    return jax.shard_map(local, mesh=mesh, in_specs=in_specs, out_specs=out_specs, check_vma=False)
```

```python
import jax
import jax.numpy as jnp
from jax import lax
from jax.experimental import pallas as pl
from jax.experimental.pallas import tpu as pltpu
from jax.sharding import PartitionSpec as P

HEADS = 64
GROUP = 128
RANK = 64
NT = 16
F = 512
O = 256
C = 1024
T = 128
ADAPTER_SCALE = 0.5
F32 = jnp.float32
BF16 = jnp.bfloat16
PARAMS = pltpu.CompilerParams(vmem_limit_bytes=24 * 1024 * 1024)
VMEM = pl.BlockSpec(memory_space=pltpu.VMEM)
SMEM = pl.BlockSpec(memory_space=pltpu.SMEM)
HBM = pl.BlockSpec(memory_space=pltpu.HBM)
DMA = pltpu.SemaphoreType.DMA


def in_hbm(*arrays):
    return [pltpu.with_memory_space_constraint(a, pltpu.HBM) for a in arrays]


def in_vmem(*arrays):
    return [pltpu.with_memory_space_constraint(a, pltpu.VMEM) for a in arrays]


def dot(a, b):
    return jnp.dot(a, b, preferred_element_type=F32)


def dot_00(a, b):
    return lax.dot_general(a, b, (((0,), (0,)), ((), ())), preferred_element_type=F32)


def dot_11(a, b):
    return lax.dot_general(a, b, (((1,), (1,)), ((), ())), preferred_element_type=F32)


def split(a):
    high = a.astype(BF16)
    return high, (a - high.astype(F32)).astype(BF16)


def butterfly(v, bits):
    n = v.shape[0]
    rest = v.shape[1:]
    for bit in range(bits):
        w = v.reshape((n >> (bit + 1), 2, 1 << bit) + rest)
        low, high = w[:, 0], w[:, 1]
        v = jnp.stack([low + high, low - high], axis=1).reshape((n,) + rest)
    return v


def iota2(shape, dim):
    return lax.broadcasted_iota(jnp.int32, shape, dim)


def weights_kernel(
    codes_hbm, scales_hbm, up_hbm, weight_out, weight_t_out, up_out,
    codes, scales, up, scales_apart, weight, weight_t, up_apart, sems, out_sems,
):
    copy_scales = pltpu.make_async_copy(scales_hbm, scales, sems.at[4])
    copy_up = pltpu.make_async_copy(up_hbm, up, sems.at[5])
    copies = []
    for g in range(4):
        rows = slice(GROUP * g, GROUP * (g + 1))
        copies.append(pltpu.make_async_copy(codes_hbm.at[rows], codes.at[rows], sems.at[g]))
    copy_scales.start()
    copy_up.start()
    for copy in copies:
        copy.start()
    row, col = iota2((512, 512), 0), iota2((512, 512), 1)
    apart = jnp.where(row == 4 * (col & 127) + (col >> 7), 1.0, 0.0).astype(BF16)
    copy_scales.wait()
    copy_up.wait()
    for block in range(8):
        lanes = slice(512 * block, 512 * (block + 1))
        s = dot(scales[:, lanes], apart)
        u = dot(up[:, lanes], apart).astype(BF16)
        for k in range(4):
            to = slice(128 * block, 128 * (block + 1))
            scales_apart[k, :, to] = s[:, 128 * k : 128 * (k + 1)]
            up_apart[k, :, to] = u[:, 128 * k : 128 * (k + 1)]
    sends = [pltpu.make_async_copy(up_apart, up_out, out_sems.at[5])]
    sends[0].start()
    for g in range(4):
        copies[g].wait()
        rows = slice(GROUP * g, GROUP * (g + 1))
        for k in range(4):
            nibble = ((codes[rows, :] >> (4 * k)) & 15) - 8
            part = nibble.astype(F32) * scales_apart[k, g : g + 1, :]
            weight[k, rows, :] = part.astype(BF16)
            weight_t[k, :, rows] = part.T.astype(BF16)
        sends.append(
            pltpu.make_async_copy(weight.at[:, rows], weight_out.at[:, rows], out_sems.at[g])
        )
        sends[g + 1].start()
    sends.append(pltpu.make_async_copy(weight_t, weight_t_out, out_sems.at[4]))
    sends[5].start()
    for send in sends:
        send.wait()


def make_weights(codes, scales, up):
    return pl.pallas_call(
        weights_kernel,
        in_specs=[HBM] * 3,
        out_specs=[HBM] * 3,
        out_shape=[
            pltpu.HBM((4, F, C), BF16),
            pltpu.HBM((4, C, F), BF16),
            pltpu.HBM((4, RANK, C), BF16),
        ],
        scratch_shapes=[
            pltpu.VMEM((F, C), jnp.int32),
            pltpu.VMEM((F // GROUP, 4 * C), BF16),
            pltpu.VMEM((RANK, 4 * C), BF16),
            pltpu.VMEM((4, F // GROUP, C), F32),
            pltpu.VMEM((4, F, C), BF16),
            pltpu.VMEM((4, C, F), BF16),
            pltpu.VMEM((4, RANK, C), BF16),
            DMA((6,)),
            DMA((6,)),
        ],
        compiler_params=PARAMS,
        cost_estimate=pl.CostEstimate(flops=20_000_000, bytes_accessed=20_000_000, transcendentals=0),
        name="weights",
    )(*in_hbm(codes, scales, up))


def pack_kernel(
    activ_hbm, flags_hbm, down_hbm, cot_hbm, sent,
    activ, flags, down_map, cot, first, own, sems, out_sems,
):
    pairs = ((activ_hbm, activ), (flags_hbm, flags), (down_hbm, down_map), (cot_hbm, cot))
    copies = [pltpu.make_async_copy(a, b, sems.at[n]) for n, (a, b) in enumerate(pairs)]
    for copy in copies:
        copy.start()
    row, col = iota2((O, O), 0), iota2((O, O), 1)
    apart = jnp.where(col == 4 * (row & 63) + (row >> 6), 1.0, 0.0).astype(BF16)
    eye = iota2((GROUP, GROUP), 0) == iota2((GROUP, GROUP), 1)
    lane, rank = iota2((RANK, 2 * RANK), 1), iota2((RANK, 2 * RANK), 0)
    left = jnp.where(lane == rank, 1.0, 0.0).astype(BF16)
    right = jnp.where(lane == rank + RANK, 1.0, 0.0).astype(BF16)
    copies[3].wait()
    own[...] = dot(apart, cot[...]).astype(BF16)
    sends = []
    for q in range(NT):
        sends.append(pltpu.make_async_copy(own, sent.at[q, 48:304], out_sems.at[q]))
        sends[q].start()
    for copy in copies[:3]:
        copy.wait()
    parts = []
    for h in range(4):
        sign = (2 * flags[h : h + 1, :] - 1).astype(F32)
        diagonal = jnp.where(eye, sign, 0.0).astype(BF16)
        parts.append(dot(diagonal, activ[GROUP * h : GROUP * (h + 1), :]).reshape(NT, 8, T))
    for h in (0, 2):
        even = down_map[:, GROUP * h : GROUP * (h + 1)]
        odd = down_map[:, GROUP * (h + 1) : GROUP * (h + 2)]
        parts.append((dot_00(even, left) + dot_00(odd, right)).reshape(NT, 8, T))
    first[...] = jnp.concatenate(parts, axis=1).astype(BF16)
    sends.append(pltpu.make_async_copy(first, sent.at[:, 0:48], out_sems.at[NT]))
    sends[NT].start()
    for send in sends:
        send.wait()


def pack(activ, flags, down_t, cot):
    return pl.pallas_call(
        pack_kernel,
        in_specs=[HBM] * 4,
        out_specs=HBM,
        out_shape=pltpu.HBM((NT, 304, T), BF16),
        scratch_shapes=[
            pltpu.VMEM((F, T), BF16),
            pltpu.VMEM((4, GROUP), jnp.int32),
            pltpu.VMEM((RANK, F), BF16),
            pltpu.VMEM((O, T), BF16),
            pltpu.VMEM((NT, 48, T), BF16),
            pltpu.VMEM((O, T), BF16),
            DMA((4,)),
            DMA((NT + 1,)),
        ],
        compiler_params=PARAMS,
        cost_estimate=pl.CostEstimate(flops=60_000_000, bytes_accessed=2_000_000, transcendentals=0),
        name="pack",
    )(*in_hbm(activ, flags, down_t, cot))


def turn_kernel(
    got, weight_hbm, up_hbm, down_hbm, sent, back_out, cot, weight, up_apart, down_t, sems
):
    copy_up = pltpu.make_async_copy(up_hbm, up_apart, sems.at[4])
    copy_down = pltpu.make_async_copy(down_hbm, down_t, sems.at[5])
    copies = []
    for h in range(4):
        rows = slice(GROUP * h, GROUP * (h + 1))
        copies.append(
            pltpu.make_async_copy(weight_hbm.at[:, rows], weight.at[:, rows], sems.at[h])
        )
    copy_up.start()
    copy_down.start()
    for copy in copies:
        copy.start()
    v = got[:, 0:32, :].astype(F32).reshape(HEADS, 8, T)
    v = butterfly(v, 6) * 0.125
    sent[:, 0:32, :] = v.reshape(NT, 32, T).astype(BF16)
    pairs = v.reshape(NT, 2, 2, 8, T)
    even = pairs[:, :, 0].reshape(256, T).astype(BF16)
    odd = pairs[:, :, 1].reshape(256, T).astype(BF16)
    maps = got[:, 32:48, :].reshape(256, 2 * RANK)
    down = dot_00(maps, even)[0:RANK] + dot_00(maps, odd)[RANK : 2 * RANK]
    down = down.astype(BF16)
    for q in range(NT):
        sent[q, 64:128, :] = down
        for k in range(4):
            cot[k, 64 * q : 64 * (q + 1), :] = got[q, 48 + 64 * k : 112 + 64 * k, :]
    copy_up.wait()
    copy_down.wait()
    back = jnp.zeros((RANK, T), F32)
    for k in range(4):
        back = back + dot(up_apart[k], cot[k])
    back_out[...] = back
    high, low = split(back)
    for h in range(4):
        rows = slice(GROUP * h, GROUP * (h + 1))
        copies[h].wait()
        maps = down_t[:, rows]
        g = ADAPTER_SCALE * (dot_00(maps, high) + dot_00(maps, low))
        for k in range(4):
            g = g + dot(weight[k, rows, :], cot[k])
        cot_rows = g.reshape(NT, 8, T)
        if h % 2 == 0:
            first = cot_rows
        else:
            both = jnp.concatenate([first, cot_rows], axis=1)
            sent[:, 24 + 8 * h : 40 + 8 * h, :] = both.astype(BF16)


def turn(got, weight, up_apart, down_t):
    return pl.pallas_call(
        turn_kernel,
        in_specs=[VMEM] + [HBM] * 3,
        out_specs=[VMEM] * 2,
        out_shape=[
            jax.ShapeDtypeStruct((NT, 128, T), BF16),
            jax.ShapeDtypeStruct((RANK, T), F32),
        ],
        scratch_shapes=[
            pltpu.VMEM((4, C, T), BF16),
            pltpu.VMEM((4, F, C), BF16),
            pltpu.VMEM((4, RANK, C), BF16),
            pltpu.VMEM((RANK, F), BF16),
            DMA((6,)),
        ],
        compiler_params=PARAMS,
        cost_estimate=pl.CostEstimate(flops=600_000_000, bytes_accessed=7_000_000, transcendentals=0),
        name="turn",
    )(got, *in_hbm(weight, up_apart, down_t))


def adapter_kernel(got, back, cot, mixed, down, sums):
    v = got[:, 0:32, :].astype(F32).reshape(NT, 4, 8, T)
    for h in range(4):
        mixed[GROUP * h : GROUP * (h + 1), :] = v[:, h].reshape(GROUP, T).astype(BF16)
    total = jnp.sum(got[:, 64:128, :].astype(F32), axis=0)
    down[...] = total
    high, low = split(total)
    back_high, back_low = split(back[...])
    for h in range(4):
        rows = slice(GROUP * h, GROUP * (h + 1))
        product = dot_11(back_high, mixed[rows, :]) + dot_11(back_low, mixed[rows, :])
        sums[RANK * h : RANK * (h + 1), :] = product
    for half in range(2):
        c = cot[GROUP * half : GROUP * (half + 1), :]
        sums[256 + RANK * half : 320 + RANK * half, :] = dot_11(high, c) + dot_11(low, c)


def adapter(got, back, cot):
    return pl.pallas_call(
        adapter_kernel,
        in_specs=[VMEM] * 3,
        out_specs=[VMEM] * 3,
        out_shape=[
            jax.ShapeDtypeStruct((F, T), BF16),
            jax.ShapeDtypeStruct((RANK, T), F32),
            jax.ShapeDtypeStruct((384, T), F32),
        ],
        compiler_params=PARAMS,
        cost_estimate=pl.CostEstimate(flops=30_000_000, bytes_accessed=1_000_000, transcendentals=0),
        name="adapter",
    )(got, back, cot)


def project_kernel(got, mixed, weight_t, sent):
    g = got[:, 32:64, :].astype(F32).reshape(HEADS, 8, T)
    g = butterfly(g, 6) * 0.125
    sent[:, 256:288, :] = g.reshape(NT, 32, T).astype(BF16)
    for k in range(4):
        share = dot(weight_t[k], mixed[...])
        sent[:, 64 * k : 64 * (k + 1), :] = share.reshape(NT, 64, T).astype(BF16)


def project(got, mixed, weight_t):
    return pl.pallas_call(
        project_kernel,
        in_specs=[VMEM] * 3,
        out_specs=VMEM,
        out_shape=jax.ShapeDtypeStruct((NT, 288, T), BF16),
        compiler_params=PARAMS,
        cost_estimate=pl.CostEstimate(flops=540_000_000, bytes_accessed=6_000_000, transcendentals=0),
        name="project",
    )(got, mixed, *in_vmem(weight_t))


def finish_kernel(place, got, up, down, flags, out, input_gradient, own, sem):
    lanes = pl.ds(pl.multiple_of(place[0] * O, O), O)
    copy = pltpu.make_async_copy(up.at[:, lanes], own, sem)
    copy.start()
    total = jnp.sum(got[:, 0:256, :].astype(F32), axis=0)
    row, col = iota2((O, O), 0), iota2((O, O), 1)
    together = jnp.where(row == 4 * (col & 63) + (col >> 6), 1.0, 0.0).astype(BF16)
    high, low = split(total)
    down_high, down_low = split(down[...])
    copy.wait()
    adapter = dot_00(own[...], down_high) + dot_00(own[...], down_low)
    out[...] = (dot(together, high) + dot(together, low) + ADAPTER_SCALE * adapter).astype(BF16)
    eye = iota2((GROUP, GROUP), 0) == iota2((GROUP, GROUP), 1)
    g = got[:, 256:288, :].astype(F32).reshape(NT, 4, 8, T)
    for h in range(4):
        sign = (2 * flags[h : h + 1, :] - 1).astype(F32)
        diagonal = jnp.where(eye, sign, 0.0).astype(BF16)
        part = g[:, h].reshape(GROUP, T).astype(BF16)
        input_gradient[GROUP * h : GROUP * (h + 1), :] = dot(diagonal, part).astype(BF16)


def finish(place, got, up, down, flags):
    return pl.pallas_call(
        finish_kernel,
        in_specs=[SMEM, VMEM, HBM, VMEM, VMEM],
        out_specs=[VMEM] * 2,
        out_shape=[
            jax.ShapeDtypeStruct((O, T), BF16),
            jax.ShapeDtypeStruct((F, T), BF16),
        ],
        scratch_shapes=[pltpu.VMEM((RANK, O), BF16), DMA(())],
        compiler_params=PARAMS,
        cost_estimate=pl.CostEstimate(flops=40_000_000, bytes_accessed=1_700_000, transcendentals=0),
        name="finish",
    )(place, got, *in_hbm(up), down, flags)


def gradients_kernel(terms, down_gradient, up_gradient):
    multiplier = ADAPTER_SCALE / 64.0
    sums = (terms[0].astype(F32) + terms[1].astype(F32)) * multiplier
    for h in range(4):
        lanes = slice(GROUP * h, GROUP * (h + 1))
        down_gradient[:, lanes] = sums[RANK * h : RANK * (h + 1), :]
    for half in range(2):
        lanes = slice(GROUP * half, GROUP * (half + 1))
        up_gradient[:, lanes] = sums[256 + RANK * half : 320 + RANK * half, :]


def gradients(terms):
    return pl.pallas_call(
        gradients_kernel,
        in_specs=[VMEM],
        out_specs=[VMEM, VMEM],
        out_shape=[
            jax.ShapeDtypeStruct((RANK, F), F32),
            jax.ShapeDtypeStruct((RANK, O), F32),
        ],
        compiler_params=PARAMS,
        cost_estimate=pl.CostEstimate(flops=100_000, bytes_accessed=500_000, transcendentals=0),
        name="gradients",
    )(terms)


def exchange(value):
    return lax.all_to_all(value, "tensor", 0, 0, tiled=True)


def terms_of(value, masks):
    devices = range(lax.axis_size("dp"))
    groups = {}
    for device in devices:
        members = [device]
        for mask in masks:
            members += [member ^ mask for member in members]
        groups[min(members)] = sorted(members)
    return lax.all_gather(
        value.astype(BF16), "dp", axis=0, axis_index_groups=list(groups.values())
    )


def sum_of(terms):
    terms = [terms[n].astype(F32) for n in range(terms.shape[0])]
    while len(terms) > 1:
        terms = [terms[n] + terms[n + 1] for n in range(0, len(terms), 2)]
    return terms[0]


def local(activ, flags, codes, scales, down_map, up, cot):
    place = jnp.stack([lax.axis_index("tensor")]).astype(jnp.int32)
    flags = flags.reshape(4, GROUP)
    down_t = down_map.T
    got = exchange(pack(activ, flags, down_t, cot))
    weight, weight_t, up_apart = make_weights(codes, scales, up)
    sent, back = turn(got, weight, up_apart, down_t)
    got = exchange(sent)
    mixed, down, sums = adapter(got, back, cot)
    got = exchange(project(got, mixed, weight_t))
    sums = sum_of(terms_of(sums, (1, 2)))
    sums = sum_of(terms_of(sums, (4,)))
    sums = sum_of(terms_of(sums, (12,)))
    terms = terms_of(sums, (16,))
    down_gradient, up_gradient = gradients(terms)
    out, input_gradient = finish(place, got, up, down, flags)
    return out, input_gradient, down_gradient.T, up_gradient


def solution(mesh):
    in_specs = (
        P("tensor", "dp"),
        P("tensor"),
        P("tensor", None),
        P("tensor", None),
        P("tensor", None),
        P(),
        P("tensor", "dp"),
    )
    out_specs = (P("tensor", "dp"), P("tensor", "dp"), P("tensor", None), P(None, "tensor"))
    return jax.shard_map(local, mesh=mesh, in_specs=in_specs, out_specs=out_specs, check_vma=False)
```

```python
import jax
import jax.numpy as jnp
from jax import lax
from jax.experimental import pallas as pl
from jax.experimental.pallas import tpu as pltpu
from jax.sharding import PartitionSpec as P

HEADS = 64
GROUP = 128
RANK = 64
NT = 16
F = 512
O = 256
C = 1024
T = 128
ADAPTER_SCALE = 0.5
F32 = jnp.float32
BF16 = jnp.bfloat16
PARAMS = pltpu.CompilerParams(vmem_limit_bytes=24 * 1024 * 1024)
VMEM = pl.BlockSpec(memory_space=pltpu.VMEM)
SMEM = pl.BlockSpec(memory_space=pltpu.SMEM)
HBM = pl.BlockSpec(memory_space=pltpu.HBM)
DMA = pltpu.SemaphoreType.DMA


def in_hbm(*arrays):
    return [pltpu.with_memory_space_constraint(a, pltpu.HBM) for a in arrays]


def in_vmem(*arrays):
    return [pltpu.with_memory_space_constraint(a, pltpu.VMEM) for a in arrays]


def dot(a, b):
    return jnp.dot(a, b, preferred_element_type=F32)


def dot_00(a, b):
    return lax.dot_general(a, b, (((0,), (0,)), ((), ())), preferred_element_type=F32)


def dot_11(a, b):
    return lax.dot_general(a, b, (((1,), (1,)), ((), ())), preferred_element_type=F32)


def split(a):
    high = a.astype(BF16)
    return high, (a - high.astype(F32)).astype(BF16)


def butterfly(v, bits):
    n = v.shape[0]
    rest = v.shape[1:]
    for bit in range(bits):
        w = v.reshape((n >> (bit + 1), 2, 1 << bit) + rest)
        low, high = w[:, 0], w[:, 1]
        v = jnp.stack([low + high, low - high], axis=1).reshape((n,) + rest)
    return v


def iota2(shape, dim):
    return lax.broadcasted_iota(jnp.int32, shape, dim)


def weights_kernel(
    codes_hbm, scales_hbm, up_hbm, weight_out, weight_t_out, up_out,
    codes, scales, up, scales_apart, weight, weight_t, up_apart, sems, out_sems,
):
    copy_scales = pltpu.make_async_copy(scales_hbm, scales, sems.at[4])
    copy_up = pltpu.make_async_copy(up_hbm, up, sems.at[5])
    copies = []
    for g in range(4):
        rows = slice(GROUP * g, GROUP * (g + 1))
        copies.append(pltpu.make_async_copy(codes_hbm.at[rows], codes.at[rows], sems.at[g]))
    copy_scales.start()
    copy_up.start()
    for copy in copies:
        copy.start()
    row, col = iota2((512, 512), 0), iota2((512, 512), 1)
    apart = jnp.where(row == 4 * (col & 127) + (col >> 7), 1.0, 0.0).astype(BF16)
    copy_scales.wait()
    copy_up.wait()
    for block in range(8):
        lanes = slice(512 * block, 512 * (block + 1))
        s = dot(scales[:, lanes], apart)
        u = dot(up[:, lanes], apart).astype(BF16)
        for k in range(4):
            to = slice(128 * block, 128 * (block + 1))
            scales_apart[k, :, to] = s[:, 128 * k : 128 * (k + 1)]
            up_apart[k, :, to] = u[:, 128 * k : 128 * (k + 1)]
    sends = [pltpu.make_async_copy(up_apart, up_out, out_sems.at[5])]
    sends[0].start()
    for g in range(4):
        copies[g].wait()
        rows = slice(GROUP * g, GROUP * (g + 1))
        for k in range(4):
            nibble = ((codes[rows, :] >> (4 * k)) & 15) - 8
            part = nibble.astype(F32) * scales_apart[k, g : g + 1, :]
            weight[k, rows, :] = part.astype(BF16)
            weight_t[k, :, rows] = part.T.astype(BF16)
        sends.append(
            pltpu.make_async_copy(weight.at[:, rows], weight_out.at[:, rows], out_sems.at[g])
        )
        sends[g + 1].start()
    sends.append(pltpu.make_async_copy(weight_t, weight_t_out, out_sems.at[4]))
    sends[5].start()
    for send in sends:
        send.wait()


def make_weights(codes, scales, up):
    return pl.pallas_call(
        weights_kernel,
        in_specs=[HBM] * 3,
        out_specs=[HBM] * 3,
        out_shape=[
            pltpu.HBM((4, F, C), BF16),
            pltpu.HBM((4, C, F), BF16),
            pltpu.HBM((4, RANK, C), BF16),
        ],
        scratch_shapes=[
            pltpu.VMEM((F, C), jnp.int32),
            pltpu.VMEM((F // GROUP, 4 * C), BF16),
            pltpu.VMEM((RANK, 4 * C), BF16),
            pltpu.VMEM((4, F // GROUP, C), F32),
            pltpu.VMEM((4, F, C), BF16),
            pltpu.VMEM((4, C, F), BF16),
            pltpu.VMEM((4, RANK, C), BF16),
            DMA((6,)),
            DMA((6,)),
        ],
        compiler_params=PARAMS,
        cost_estimate=pl.CostEstimate(flops=20_000_000, bytes_accessed=20_000_000, transcendentals=0),
        name="weights",
    )(*in_hbm(codes, scales, up))


def pack_kernel(
    activ_hbm, flags_hbm, down_hbm, cot_hbm, sent,
    activ, flags, down_map, cot, first, own, sems, out_sems,
):
    pairs = ((activ_hbm, activ), (flags_hbm, flags), (down_hbm, down_map), (cot_hbm, cot))
    copies = [pltpu.make_async_copy(a, b, sems.at[n]) for n, (a, b) in enumerate(pairs)]
    for copy in copies:
        copy.start()
    row, col = iota2((O, O), 0), iota2((O, O), 1)
    apart = jnp.where(col == 4 * (row & 63) + (row >> 6), 1.0, 0.0).astype(BF16)
    eye = iota2((GROUP, GROUP), 0) == iota2((GROUP, GROUP), 1)
    lane, rank = iota2((RANK, 2 * RANK), 1), iota2((RANK, 2 * RANK), 0)
    left = jnp.where(lane == rank, 1.0, 0.0).astype(BF16)
    right = jnp.where(lane == rank + RANK, 1.0, 0.0).astype(BF16)
    copies[3].wait()
    own[...] = dot(apart, cot[...]).astype(BF16)
    sends = []
    for q in range(NT):
        sends.append(pltpu.make_async_copy(own, sent.at[q, 48:304], out_sems.at[q]))
        sends[q].start()
    for copy in copies[:3]:
        copy.wait()
    parts = []
    for h in range(4):
        sign = (2 * flags[h : h + 1, :] - 1).astype(F32)
        diagonal = jnp.where(eye, sign, 0.0).astype(BF16)
        parts.append(dot(diagonal, activ[GROUP * h : GROUP * (h + 1), :]).reshape(NT, 8, T))
    for h in (0, 2):
        even = down_map[:, GROUP * h : GROUP * (h + 1)]
        odd = down_map[:, GROUP * (h + 1) : GROUP * (h + 2)]
        parts.append((dot_00(even, left) + dot_00(odd, right)).reshape(NT, 8, T))
    first[...] = jnp.concatenate(parts, axis=1).astype(BF16)
    sends.append(pltpu.make_async_copy(first, sent.at[:, 0:48], out_sems.at[NT]))
    sends[NT].start()
    for send in sends:
        send.wait()


def pack(activ, flags, down_t, cot):
    return pl.pallas_call(
        pack_kernel,
        in_specs=[HBM] * 4,
        out_specs=HBM,
        out_shape=pltpu.HBM((NT, 304, T), BF16),
        scratch_shapes=[
            pltpu.VMEM((F, T), BF16),
            pltpu.VMEM((4, GROUP), jnp.int32),
            pltpu.VMEM((RANK, F), BF16),
            pltpu.VMEM((O, T), BF16),
            pltpu.VMEM((NT, 48, T), BF16),
            pltpu.VMEM((O, T), BF16),
            DMA((4,)),
            DMA((NT + 1,)),
        ],
        compiler_params=PARAMS,
        cost_estimate=pl.CostEstimate(flops=60_000_000, bytes_accessed=2_000_000, transcendentals=0),
        name="pack",
    )(*in_hbm(activ, flags, down_t, cot))


def turn_kernel(
    got, weight_hbm, up_hbm, down_hbm, sent, back_out, cot, weight, up_apart, down_t, sems
):
    copy_up = pltpu.make_async_copy(up_hbm, up_apart, sems.at[4])
    copy_down = pltpu.make_async_copy(down_hbm, down_t, sems.at[5])
    copies = []
    for h in range(4):
        rows = slice(GROUP * h, GROUP * (h + 1))
        copies.append(
            pltpu.make_async_copy(weight_hbm.at[:, rows], weight.at[:, rows], sems.at[h])
        )
    copy_up.start()
    copy_down.start()
    for copy in copies:
        copy.start()
    v = got[:, 0:32, :].astype(F32).reshape(HEADS, 8, T)
    v = butterfly(v, 6) * 0.125
    sent[:, 0:32, :] = v.reshape(NT, 32, T).astype(BF16)
    pairs = v.reshape(NT, 2, 2, 8, T)
    even = pairs[:, :, 0].reshape(256, T).astype(BF16)
    odd = pairs[:, :, 1].reshape(256, T).astype(BF16)
    maps = got[:, 32:48, :].reshape(256, 2 * RANK)
    down = dot_00(maps, even)[0:RANK] + dot_00(maps, odd)[RANK : 2 * RANK]
    down = down.astype(BF16)
    for q in range(NT):
        sent[q, 64:128, :] = down
        for k in range(4):
            cot[k, 64 * q : 64 * (q + 1), :] = got[q, 48 + 64 * k : 112 + 64 * k, :]
    copy_up.wait()
    copy_down.wait()
    back = jnp.zeros((RANK, T), F32)
    for k in range(4):
        back = back + dot(up_apart[k], cot[k])
    back_out[...] = back
    high, low = split(back)
    for h in range(4):
        rows = slice(GROUP * h, GROUP * (h + 1))
        copies[h].wait()
        maps = down_t[:, rows]
        g = ADAPTER_SCALE * (dot_00(maps, high) + dot_00(maps, low))
        for k in range(4):
            g = g + dot(weight[k, rows, :], cot[k])
        cot_rows = g.reshape(NT, 8, T)
        if h % 2 == 0:
            first = cot_rows
        else:
            both = jnp.concatenate([first, cot_rows], axis=1)
            sent[:, 24 + 8 * h : 40 + 8 * h, :] = both.astype(BF16)


def turn(got, weight, up_apart, down_t):
    return pl.pallas_call(
        turn_kernel,
        in_specs=[VMEM] + [HBM] * 3,
        out_specs=[VMEM] * 2,
        out_shape=[
            jax.ShapeDtypeStruct((NT, 128, T), BF16),
            jax.ShapeDtypeStruct((RANK, T), F32),
        ],
        scratch_shapes=[
            pltpu.VMEM((4, C, T), BF16),
            pltpu.VMEM((4, F, C), BF16),
            pltpu.VMEM((4, RANK, C), BF16),
            pltpu.VMEM((RANK, F), BF16),
            DMA((6,)),
        ],
        compiler_params=PARAMS,
        cost_estimate=pl.CostEstimate(flops=600_000_000, bytes_accessed=7_000_000, transcendentals=0),
        name="turn",
    )(got, *in_hbm(weight, up_apart, down_t))


def adapter_kernel(got, back, cot, mixed, down, sums):
    v = got[:, 0:32, :].astype(F32).reshape(NT, 4, 8, T)
    for h in range(4):
        mixed[GROUP * h : GROUP * (h + 1), :] = v[:, h].reshape(GROUP, T).astype(BF16)
    total = jnp.sum(got[:, 64:128, :].astype(F32), axis=0)
    down[...] = total
    high, low = split(total)
    back_high, back_low = split(back[...])
    for h in range(4):
        rows = slice(GROUP * h, GROUP * (h + 1))
        product = dot_11(back_high, mixed[rows, :]) + dot_11(back_low, mixed[rows, :])
        sums[RANK * h : RANK * (h + 1), :] = product
    for half in range(2):
        c = cot[GROUP * half : GROUP * (half + 1), :]
        sums[256 + RANK * half : 320 + RANK * half, :] = dot_11(high, c) + dot_11(low, c)


def adapter(got, back, cot):
    return pl.pallas_call(
        adapter_kernel,
        in_specs=[VMEM] * 3,
        out_specs=[VMEM] * 3,
        out_shape=[
            jax.ShapeDtypeStruct((F, T), BF16),
            jax.ShapeDtypeStruct((RANK, T), F32),
            jax.ShapeDtypeStruct((384, T), F32),
        ],
        compiler_params=PARAMS,
        cost_estimate=pl.CostEstimate(flops=30_000_000, bytes_accessed=1_000_000, transcendentals=0),
        name="adapter",
    )(got, back, cot)


def project_kernel(got, mixed, weight_t, sent):
    g = got[:, 32:64, :].astype(F32).reshape(HEADS, 8, T)
    g = butterfly(g, 6) * 0.125
    sent[:, 256:288, :] = g.reshape(NT, 32, T).astype(BF16)
    for k in range(4):
        share = dot(weight_t[k], mixed[...])
        sent[:, 64 * k : 64 * (k + 1), :] = share.reshape(NT, 64, T).astype(BF16)


def project(got, mixed, weight_t):
    return pl.pallas_call(
        project_kernel,
        in_specs=[VMEM] * 3,
        out_specs=VMEM,
        out_shape=jax.ShapeDtypeStruct((NT, 288, T), BF16),
        compiler_params=PARAMS,
        cost_estimate=pl.CostEstimate(flops=540_000_000, bytes_accessed=6_000_000, transcendentals=0),
        name="project",
    )(got, mixed, *in_vmem(weight_t))


def finish_kernel(place, got, up, down, flags, out, input_gradient, own, sem):
    lanes = pl.ds(pl.multiple_of(place[0] * O, O), O)
    copy = pltpu.make_async_copy(up.at[:, lanes], own, sem)
    copy.start()
    total = jnp.sum(got[:, 0:256, :].astype(F32), axis=0)
    row, col = iota2((O, O), 0), iota2((O, O), 1)
    together = jnp.where(row == 4 * (col & 63) + (col >> 6), 1.0, 0.0).astype(BF16)
    high, low = split(total)
    down_high, down_low = split(down[...])
    copy.wait()
    adapter = dot_00(own[...], down_high) + dot_00(own[...], down_low)
    out[...] = (dot(together, high) + dot(together, low) + ADAPTER_SCALE * adapter).astype(BF16)
    eye = iota2((GROUP, GROUP), 0) == iota2((GROUP, GROUP), 1)
    g = got[:, 256:288, :].astype(F32).reshape(NT, 4, 8, T)
    for h in range(4):
        sign = (2 * flags[h : h + 1, :] - 1).astype(F32)
        diagonal = jnp.where(eye, sign, 0.0).astype(BF16)
        part = g[:, h].reshape(GROUP, T).astype(BF16)
        input_gradient[GROUP * h : GROUP * (h + 1), :] = dot(diagonal, part).astype(BF16)


def finish(place, got, up, down, flags):
    return pl.pallas_call(
        finish_kernel,
        in_specs=[SMEM, VMEM, HBM, VMEM, VMEM],
        out_specs=[VMEM] * 2,
        out_shape=[
            jax.ShapeDtypeStruct((O, T), BF16),
            jax.ShapeDtypeStruct((F, T), BF16),
        ],
        scratch_shapes=[pltpu.VMEM((RANK, O), BF16), DMA(())],
        compiler_params=PARAMS,
        cost_estimate=pl.CostEstimate(flops=40_000_000, bytes_accessed=1_700_000, transcendentals=0),
        name="finish",
    )(place, got, *in_hbm(up), down, flags)


def gradients_kernel(sums, down_gradient, up_gradient):
    multiplier = ADAPTER_SCALE / 64.0
    for h in range(4):
        lanes = slice(GROUP * h, GROUP * (h + 1))
        down_gradient[:, lanes] = sums[RANK * h : RANK * (h + 1), :] * multiplier
    for half in range(2):
        lanes = slice(GROUP * half, GROUP * (half + 1))
        up_gradient[:, lanes] = sums[256 + RANK * half : 320 + RANK * half, :] * multiplier


def gradients(sums):
    return pl.pallas_call(
        gradients_kernel,
        in_specs=[VMEM],
        out_specs=[VMEM, VMEM],
        out_shape=[
            jax.ShapeDtypeStruct((RANK, F), F32),
            jax.ShapeDtypeStruct((RANK, O), F32),
        ],
        compiler_params=PARAMS,
        cost_estimate=pl.CostEstimate(flops=100_000, bytes_accessed=500_000, transcendentals=0),
        name="gradients",
    )(sums)


def exchange(value):
    return lax.all_to_all(value, "tensor", 0, 0, tiled=True)


def gather(value, masks):
    groups = {}
    for device in range(lax.axis_size("dp")):
        members = [device]
        for mask in masks:
            members += [member ^ mask for member in members]
        groups[min(members)] = sorted(members)
    return lax.all_gather(value, "dp", axis=0, axis_index_groups=list(groups.values()))


def sum_over(value, masks):
    terms = gather(value.astype(BF16), masks)
    terms = [terms[n].astype(F32) for n in range(terms.shape[0])]
    while len(terms) > 1:
        terms = [terms[n] + terms[n + 1] for n in range(0, len(terms), 2)]
    return terms[0]


def local(activ, flags, codes, scales, down_map, up, cot):
    replica = lax.axis_index("dp")
    place = jnp.stack([lax.axis_index("tensor")]).astype(jnp.int32)
    flags = flags.reshape(4, GROUP)
    down_t = down_map.T
    got = exchange(pack(activ, flags, down_t, cot))
    weight, weight_t, up_apart = make_weights(codes, scales, up)
    sent, back = turn(got, weight, up_apart, down_t)
    got = exchange(sent)
    mixed, down, sums = adapter(got, back, cot)
    got = exchange(project(got, mixed, weight_t))
    half = lax.dynamic_slice_in_dim(sum_over(sums, (1, 2)), 192 * (replica & 1), 192)
    half = sum_over(half, (4,))
    half = sum_over(half, (12,)).astype(BF16)
    pairs = [(source, source ^ 16) for source in range(lax.axis_size("dp"))]
    other = lax.ppermute(half, "dp", pairs)
    out, input_gradient = finish(place, got, up, down, flags)
    other, out, input_gradient = lax.optimization_barrier((other, out, input_gradient))
    half = half.astype(F32) + other.astype(F32)
    down_gradient, up_gradient = gradients(gather(half, (1,)).reshape(384, T))
    return out, input_gradient, down_gradient.T, up_gradient


def solution(mesh):
    in_specs = (
        P("tensor", "dp"),
        P("tensor"),
        P("tensor", None),
        P("tensor", None),
        P("tensor", None),
        P(),
        P("tensor", "dp"),
    )
    out_specs = (P("tensor", "dp"), P("tensor", "dp"), P("tensor", None), P(None, "tensor"))
    return jax.shard_map(local, mesh=mesh, in_specs=in_specs, out_specs=out_specs, check_vma=False)
```

```python
import jax
import jax.numpy as jnp
from jax import lax
from jax.experimental import pallas as pl
from jax.experimental.pallas import tpu as pltpu
from jax.sharding import PartitionSpec as P

HEADS = 64
GROUP = 128
RANK = 64
NT = 16
F = 512
O = 256
C = 1024
T = 128
ADAPTER_SCALE = 0.5
F32 = jnp.float32
BF16 = jnp.bfloat16
PARAMS = pltpu.CompilerParams(vmem_limit_bytes=24 * 1024 * 1024)
VMEM = pl.BlockSpec(memory_space=pltpu.VMEM)
SMEM = pl.BlockSpec(memory_space=pltpu.SMEM)
HBM = pl.BlockSpec(memory_space=pltpu.HBM)
DMA = pltpu.SemaphoreType.DMA


def in_hbm(*arrays):
    return [pltpu.with_memory_space_constraint(a, pltpu.HBM) for a in arrays]


def in_vmem(*arrays):
    return [pltpu.with_memory_space_constraint(a, pltpu.VMEM) for a in arrays]


def dot(a, b):
    return jnp.dot(a, b, preferred_element_type=F32)


def dot_00(a, b):
    return lax.dot_general(a, b, (((0,), (0,)), ((), ())), preferred_element_type=F32)


def dot_11(a, b):
    return lax.dot_general(a, b, (((1,), (1,)), ((), ())), preferred_element_type=F32)


def split(a):
    high = a.astype(BF16)
    return high, (a - high.astype(F32)).astype(BF16)


def butterfly(v, bits):
    n = v.shape[0]
    rest = v.shape[1:]
    for bit in range(bits):
        w = v.reshape((n >> (bit + 1), 2, 1 << bit) + rest)
        low, high = w[:, 0], w[:, 1]
        v = jnp.stack([low + high, low - high], axis=1).reshape((n,) + rest)
    return v


def iota2(shape, dim):
    return lax.broadcasted_iota(jnp.int32, shape, dim)


def weights_kernel(
    codes_hbm, scales_hbm, up_hbm, weight_out, up_out,
    codes, scales, up, scales_apart, weight, up_apart, sems, out_sems,
):
    copy_scales = pltpu.make_async_copy(scales_hbm, scales, sems.at[4])
    copy_up = pltpu.make_async_copy(up_hbm, up, sems.at[5])
    copies = []
    for g in range(4):
        rows = slice(GROUP * g, GROUP * (g + 1))
        copies.append(pltpu.make_async_copy(codes_hbm.at[rows], codes.at[rows], sems.at[g]))
    copy_scales.start()
    copy_up.start()
    for copy in copies:
        copy.start()
    row, col = iota2((512, 512), 0), iota2((512, 512), 1)
    apart = jnp.where(row == 4 * (col & 127) + (col >> 7), 1.0, 0.0).astype(BF16)
    copy_scales.wait()
    copy_up.wait()
    for block in range(8):
        lanes = slice(512 * block, 512 * (block + 1))
        s = dot(scales[:, lanes], apart)
        u = dot(up[:, lanes], apart).astype(BF16)
        for k in range(4):
            to = slice(128 * block, 128 * (block + 1))
            scales_apart[k, :, to] = s[:, 128 * k : 128 * (k + 1)]
            up_apart[k, :, to] = u[:, 128 * k : 128 * (k + 1)]
    sends = [pltpu.make_async_copy(up_apart, up_out, out_sems.at[5])]
    sends[0].start()
    for g in range(4):
        copies[g].wait()
        rows = slice(GROUP * g, GROUP * (g + 1))
        for k in range(4):
            nibble = ((codes[rows, :] >> (4 * k)) & 15) - 8
            part = nibble.astype(F32) * scales_apart[k, g : g + 1, :]
            weight[k, rows, :] = part.astype(BF16)
        sends.append(
            pltpu.make_async_copy(weight.at[:, rows], weight_out.at[:, rows], out_sems.at[g])
        )
        sends[g + 1].start()
    for send in sends:
        send.wait()


def make_weights(codes, scales, up):
    return pl.pallas_call(
        weights_kernel,
        in_specs=[HBM] * 3,
        out_specs=[HBM] * 2,
        out_shape=[
            pltpu.HBM((4, F, C), BF16),
            pltpu.HBM((4, RANK, C), BF16),
        ],
        scratch_shapes=[
            pltpu.VMEM((F, C), jnp.int32),
            pltpu.VMEM((F // GROUP, 4 * C), BF16),
            pltpu.VMEM((RANK, 4 * C), BF16),
            pltpu.VMEM((4, F // GROUP, C), F32),
            pltpu.VMEM((4, F, C), BF16),
            pltpu.VMEM((4, RANK, C), BF16),
            DMA((6,)),
            DMA((6,)),
        ],
        compiler_params=PARAMS,
        cost_estimate=pl.CostEstimate(flops=20_000_000, bytes_accessed=20_000_000, transcendentals=0),
        name="weights",
    )(*in_hbm(codes, scales, up))


def lanes_in_order(value):
    halves = value.reshape(2, 8, 8, T)
    return jnp.stack([halves[0], halves[1]], axis=1).reshape(GROUP, T)


def lanes_by_device(value):
    value = value.reshape(8, 2, 8, T)
    return jnp.concatenate([value[:, 0], value[:, 1]], axis=0)


def sign_kernel(
    place, activ_hbm, flags_hbm, down_hbm, cot_hbm, keep, give, activ, flags, down_map, cot, sems
):
    pairs = ((activ_hbm, activ), (flags_hbm, flags), (down_hbm, down_map), (cot_hbm, cot))
    copies = [pltpu.make_async_copy(a, b, sems.at[n]) for n, (a, b) in enumerate(pairs)]
    for copy in copies:
        copy.start()
    row, col = iota2((O, O), 0), iota2((O, O), 1)
    apart = jnp.where(col == 4 * (row & 63) + (row >> 6), 1.0, 0.0).astype(BF16)
    eye = iota2((GROUP, GROUP), 0) == iota2((GROUP, GROUP), 1)
    lane, rank = iota2((RANK, 2 * RANK), 1), iota2((RANK, 2 * RANK), 0)
    left = jnp.where(lane == rank, 1.0, 0.0).astype(BF16)
    right = jnp.where(lane == rank + RANK, 1.0, 0.0).astype(BF16)
    for copy in copies:
        copy.wait()
    parts = []
    for h in range(4):
        sign = (2 * flags[h : h + 1, :] - 1).astype(F32)
        diagonal = jnp.where(eye, sign, 0.0).astype(BF16)
        parts.append(dot(diagonal, activ[GROUP * h : GROUP * (h + 1), :]))
    for h in (0, 2):
        even = down_map[:, GROUP * h : GROUP * (h + 1)]
        odd = down_map[:, GROUP * (h + 1) : GROUP * (h + 2)]
        parts.append(dot_00(even, left) + dot_00(odd, right))
    parts = [part.reshape(8, 2, 8, T) for part in parts]
    low, high = (
        jnp.concatenate([part[:, n] for part in parts], axis=1).reshape(384, T) for n in range(2)
    )
    keep[0:384, :] = jnp.where(place[1] == 0, low, high).astype(BF16)
    give[0:384, :] = jnp.where(place[1] == 0, high, low).astype(BF16)
    own = dot(apart, cot[...]).astype(BF16)
    keep[384:640, :] = own
    give[384:640, :] = own


def sign(place, activ, flags, down_t, cot):
    return pl.pallas_call(
        sign_kernel,
        in_specs=[SMEM] + [HBM] * 4,
        out_specs=[VMEM] * 2,
        out_shape=[jax.ShapeDtypeStruct((640, T), BF16)] * 2,
        scratch_shapes=[
            pltpu.VMEM((F, T), BF16),
            pltpu.VMEM((4, GROUP), jnp.int32),
            pltpu.VMEM((RANK, F), BF16),
            pltpu.VMEM((O, T), BF16),
            DMA((4,)),
        ],
        compiler_params=PARAMS,
        cost_estimate=pl.CostEstimate(flops=60_000_000, bytes_accessed=600_000, transcendentals=0),
        name="sign",
    )(place, *in_hbm(activ, flags, down_t, cot))


def pack_kernel(own, other, sent):
    for n, part in enumerate((own, other)):
        cot = part[384:640, :]
        for j in range(8):
            sent[j, 48 * n : 48 * (n + 1), :] = part[48 * j : 48 * (j + 1), :]
            sent[j, 96 + 256 * n : 352 + 256 * n, :] = cot


def pack(own, other):
    return pl.pallas_call(
        pack_kernel,
        in_specs=[VMEM] * 2,
        out_specs=VMEM,
        out_shape=pltpu.VMEM((8, 608, T), BF16),
        compiler_params=PARAMS,
        cost_estimate=pl.CostEstimate(flops=0, bytes_accessed=2_000_000, transcendentals=0),
        name="pack",
    )(own, other)


def turn_kernel(
    place, got, weight_hbm, up_hbm, down_hbm, sent, back_out,
    cot, weight, up_apart, down_t, sems,
):
    copy_up = pltpu.make_async_copy(up_hbm, up_apart, sems.at[4])
    copy_down = pltpu.make_async_copy(down_hbm, down_t, sems.at[5])
    copies = []
    for h in range(4):
        rows = slice(GROUP * h, GROUP * (h + 1))
        copies.append(
            pltpu.make_async_copy(weight_hbm.at[:, rows], weight.at[:, rows], sems.at[h])
        )
    copy_up.start()
    copy_down.start()
    for copy in copies:
        copy.start()
    one, two = got[:, 0:48, :].astype(F32), got[:, 48:96, :].astype(F32)
    low = jnp.where(place[1] == 0, one, two)
    high = jnp.where(place[1] == 0, two, one)
    both = jnp.concatenate([low, high], axis=0)
    v = butterfly(both[:, 0:32].reshape(HEADS, 8, T), 6) * 0.125
    sent[:, 0:32, :] = v.reshape(NT, 32, T).astype(BF16)
    pairs = v.reshape(NT, 2, 2, 8, T)
    even = pairs[:, :, 0].reshape(256, T).astype(BF16)
    odd = pairs[:, :, 1].reshape(256, T).astype(BF16)
    maps = both[:, 32:48].reshape(256, 2 * RANK).astype(BF16)
    down = dot_00(maps, even)[0:RANK] + dot_00(maps, odd)[RANK : 2 * RANK]
    down = down.astype(BF16)
    for q in range(NT):
        sent[q, 64:128, :] = down
    for n in range(2):
        start = 512 * (place[1] ^ n)
        for j in range(8):
            rows = pl.ds(pl.multiple_of(start + 64 * j, 64), 64)
            for k in range(4):
                at = 96 + 256 * n + 64 * k
                cot[k, rows, :] = got[j, at : at + 64, :]
    copy_up.wait()
    copy_down.wait()
    back = jnp.zeros((RANK, T), F32)
    for k in range(4):
        back = back + dot(up_apart[k], cot[k])
    back_out[...] = back
    high, low = split(back)
    for h in range(4):
        rows = slice(GROUP * h, GROUP * (h + 1))
        copies[h].wait()
        maps = down_t[:, rows]
        g = ADAPTER_SCALE * (dot_00(maps, high) + dot_00(maps, low))
        for k in range(4):
            g = g + dot(weight[k, rows, :], cot[k])
        g = lanes_by_device(g)
        if h % 2 == 0:
            first = g
        else:
            both = jnp.concatenate([first, g], axis=1)
            sent[:, 24 + 8 * h : 40 + 8 * h, :] = both.astype(BF16)


def turn(place, got, weight, up_apart, down_t):
    return pl.pallas_call(
        turn_kernel,
        in_specs=[SMEM, VMEM] + [HBM] * 3,
        out_specs=[VMEM] * 2,
        out_shape=[
            jax.ShapeDtypeStruct((NT, 128, T), BF16),
            jax.ShapeDtypeStruct((RANK, T), F32),
        ],
        scratch_shapes=[
            pltpu.VMEM((4, C, T), BF16),
            pltpu.VMEM((4, F, C), BF16),
            pltpu.VMEM((4, RANK, C), BF16),
            pltpu.VMEM((RANK, F), BF16),
            DMA((6,)),
        ],
        compiler_params=PARAMS,
        cost_estimate=pl.CostEstimate(flops=600_000_000, bytes_accessed=7_000_000, transcendentals=0),
        name="turn",
    )(place, got, *in_hbm(weight, up_apart, down_t))


def adapter_kernel(got, mixed, back, cot, down, sums):
    total = jnp.sum(got[:, 64:128, :].astype(F32), axis=0)
    down[...] = total
    high, low = split(total)
    back_high, back_low = split(back[...])
    for h in range(4):
        rows = slice(GROUP * h, GROUP * (h + 1))
        product = dot_11(back_high, mixed[rows, :]) + dot_11(back_low, mixed[rows, :])
        sums[RANK * h : RANK * (h + 1), :] = product
    for half in range(2):
        c = cot[GROUP * half : GROUP * (half + 1), :]
        sums[256 + RANK * half : 320 + RANK * half, :] = dot_11(high, c) + dot_11(low, c)


def adapter(got, mixed, back, cot):
    return pl.pallas_call(
        adapter_kernel,
        in_specs=[VMEM] * 4,
        out_specs=[VMEM] * 2,
        out_shape=[
            jax.ShapeDtypeStruct((RANK, T), F32),
            jax.ShapeDtypeStruct((384, T), F32),
        ],
        compiler_params=PARAMS,
        cost_estimate=pl.CostEstimate(flops=30_000_000, bytes_accessed=1_000_000, transcendentals=0),
        name="adapter",
    )(got, mixed, back, cot)


def project_kernel(got, weight, sent, mixed):
    v = got[:, 0:32, :].astype(F32).reshape(NT, 4, 8, T)
    for h in range(4):
        mixed[GROUP * h : GROUP * (h + 1), :] = lanes_in_order(v[:, h]).astype(BF16)
    g = got[:, 32:64, :].astype(F32).reshape(HEADS, 8, T)
    g = butterfly(g, 6) * 0.125
    sent[:, 256:288, :] = g.reshape(NT, 32, T).astype(BF16)
    for k in range(4):
        share = dot_00(weight[k], mixed[...])
        sent[:, 64 * k : 64 * (k + 1), :] = share.reshape(NT, 64, T).astype(BF16)


def project(got, weight):
    return pl.pallas_call(
        project_kernel,
        in_specs=[VMEM] * 2,
        out_specs=[VMEM] * 2,
        out_shape=[
            jax.ShapeDtypeStruct((NT, 288, T), BF16),
            jax.ShapeDtypeStruct((F, T), BF16),
        ],
        compiler_params=PARAMS,
        cost_estimate=pl.CostEstimate(flops=540_000_000, bytes_accessed=6_000_000, transcendentals=0),
        name="project",
    )(got, *in_vmem(weight))


def finish_kernel(place, got, up, down, flags, out, input_gradient, own, sem):
    lanes = pl.ds(pl.multiple_of(place[0] * O, O), O)
    copy = pltpu.make_async_copy(up.at[:, lanes], own, sem)
    copy.start()
    total = jnp.sum(got[:, 0:256, :].astype(F32), axis=0)
    row, col = iota2((O, O), 0), iota2((O, O), 1)
    together = jnp.where(row == 4 * (col & 63) + (col >> 6), 1.0, 0.0).astype(BF16)
    high, low = split(total)
    down_high, down_low = split(down[...])
    copy.wait()
    adapter = dot_00(own[...], down_high) + dot_00(own[...], down_low)
    out[...] = (dot(together, high) + dot(together, low) + ADAPTER_SCALE * adapter).astype(BF16)
    eye = iota2((GROUP, GROUP), 0) == iota2((GROUP, GROUP), 1)
    g = got[:, 256:288, :].astype(F32).reshape(NT, 4, 8, T)
    for h in range(4):
        sign = (2 * flags[h : h + 1, :] - 1).astype(F32)
        diagonal = jnp.where(eye, sign, 0.0).astype(BF16)
        part = lanes_in_order(g[:, h]).astype(BF16)
        input_gradient[GROUP * h : GROUP * (h + 1), :] = dot(diagonal, part).astype(BF16)


def finish(place, got, up, down, flags):
    return pl.pallas_call(
        finish_kernel,
        in_specs=[SMEM, VMEM, HBM, VMEM, VMEM],
        out_specs=[VMEM] * 2,
        out_shape=[
            jax.ShapeDtypeStruct((O, T), BF16),
            jax.ShapeDtypeStruct((F, T), BF16),
        ],
        scratch_shapes=[pltpu.VMEM((RANK, O), BF16), DMA(())],
        compiler_params=PARAMS,
        cost_estimate=pl.CostEstimate(flops=40_000_000, bytes_accessed=1_700_000, transcendentals=0),
        name="finish",
    )(place, got, *in_hbm(up), down, flags)


def gradients_kernel(sums, down_gradient, up_gradient):
    multiplier = ADAPTER_SCALE / 64.0
    for h in range(4):
        lanes = slice(GROUP * h, GROUP * (h + 1))
        down_gradient[:, lanes] = sums[RANK * h : RANK * (h + 1), :] * multiplier
    for half in range(2):
        lanes = slice(GROUP * half, GROUP * (half + 1))
        up_gradient[:, lanes] = sums[256 + RANK * half : 320 + RANK * half, :] * multiplier


def gradients(sums):
    return pl.pallas_call(
        gradients_kernel,
        in_specs=[VMEM],
        out_specs=[VMEM, VMEM],
        out_shape=[
            jax.ShapeDtypeStruct((RANK, F), F32),
            jax.ShapeDtypeStruct((RANK, O), F32),
        ],
        compiler_params=PARAMS,
        cost_estimate=pl.CostEstimate(flops=100_000, bytes_accessed=500_000, transcendentals=0),
        name="gradients",
    )(sums)


def exchange(value):
    return lax.all_to_all(value, "tensor", 0, 0, tiled=True)


def gather(value, masks):
    groups = {}
    for device in range(lax.axis_size("dp")):
        members = [device]
        for mask in masks:
            members += [member ^ mask for member in members]
        groups[min(members)] = sorted(members)
    return lax.all_gather(value, "dp", axis=0, axis_index_groups=list(groups.values()))


def sum_over(value, masks):
    terms = gather(value.astype(BF16), masks)
    terms = [terms[n].astype(F32) for n in range(terms.shape[0])]
    while len(terms) > 1:
        terms = [terms[n] + terms[n + 1] for n in range(0, len(terms), 2)]
    return terms[0]


def local(activ, flags, codes, scales, down_map, up, cot):
    replica = lax.axis_index("dp")
    me = lax.axis_index("tensor")
    place = jnp.stack([me, me >> 3]).astype(jnp.int32)
    flags = flags.reshape(4, GROUP)
    down_t = down_map.T
    own, give = sign(place, activ, flags, down_t, cot)
    other = lax.ppermute(give, "tensor", [(source, source ^ 8) for source in range(NT)])
    weight, up_apart = make_weights(codes, scales, up)
    other, weight = lax.optimization_barrier((other, weight))
    halves = [list(range(8)), list(range(8, NT))]
    got = lax.all_to_all(
        pack(own, other), "tensor", 0, 0, tiled=True, axis_index_groups=halves
    )
    sent, back = turn(place, got, weight, up_apart, down_t)
    got = exchange(sent)
    sent, mixed = project(got, weight)
    down, sums = adapter(got, mixed, back, cot)
    got = exchange(sent)
    half = lax.dynamic_slice_in_dim(sum_over(sums, (1, 2)), 192 * (replica & 1), 192)
    half = sum_over(half, (4,))
    half = sum_over(half, (12,)).astype(BF16)
    pairs = [(source, source ^ 16) for source in range(lax.axis_size("dp"))]
    other = lax.ppermute(half, "dp", pairs)
    out, input_gradient = finish(place, got, up, down, flags)
    other, out, input_gradient = lax.optimization_barrier((other, out, input_gradient))
    half = half.astype(F32) + other.astype(F32)
    down_gradient, up_gradient = gradients(gather(half, (1,)).reshape(384, T))
    return out, input_gradient, down_gradient.T, up_gradient


def solution(mesh):
    in_specs = (
        P("tensor", "dp"),
        P("tensor"),
        P("tensor", None),
        P("tensor", None),
        P("tensor", None),
        P(),
        P("tensor", "dp"),
    )
    out_specs = (P("tensor", "dp"), P("tensor", "dp"), P("tensor", None), P(None, "tensor"))
    return jax.shard_map(local, mesh=mesh, in_specs=in_specs, out_specs=out_specs, check_vma=False)
```

```python
import jax
import jax.numpy as jnp
from jax import lax
from jax.experimental import pallas as pl
from jax.experimental.pallas import tpu as pltpu
from jax.sharding import PartitionSpec as P

HEADS = 64
GROUP = 128
RANK = 64
NT = 16
F = 512
O = 256
C = 1024
T = 128
ADAPTER_SCALE = 0.5
F32 = jnp.float32
BF16 = jnp.bfloat16
PARAMS = pltpu.CompilerParams(vmem_limit_bytes=24 * 1024 * 1024)
VMEM = pl.BlockSpec(memory_space=pltpu.VMEM)
SMEM = pl.BlockSpec(memory_space=pltpu.SMEM)
HBM = pl.BlockSpec(memory_space=pltpu.HBM)
DMA = pltpu.SemaphoreType.DMA


def in_hbm(*arrays):
    return [pltpu.with_memory_space_constraint(a, pltpu.HBM) for a in arrays]


def in_vmem(*arrays):
    return [pltpu.with_memory_space_constraint(a, pltpu.VMEM) for a in arrays]


def dot(a, b):
    return jnp.dot(a, b, preferred_element_type=F32)


def dot_00(a, b):
    return lax.dot_general(a, b, (((0,), (0,)), ((), ())), preferred_element_type=F32)


def dot_11(a, b):
    return lax.dot_general(a, b, (((1,), (1,)), ((), ())), preferred_element_type=F32)


def split(a):
    high = a.astype(BF16)
    return high, (a - high.astype(F32)).astype(BF16)


def butterfly(v, bits):
    n = v.shape[0]
    rest = v.shape[1:]
    for bit in range(bits):
        w = v.reshape((n >> (bit + 1), 2, 1 << bit) + rest)
        low, high = w[:, 0], w[:, 1]
        v = jnp.stack([low + high, low - high], axis=1).reshape((n,) + rest)
    return v


def iota2(shape, dim):
    return lax.broadcasted_iota(jnp.int32, shape, dim)


def weights_kernel(
    codes_hbm, scales_hbm, up_hbm, weight, up_apart,
    codes, scales, up, scales_apart, sems,
):
    copy_scales = pltpu.make_async_copy(scales_hbm, scales, sems.at[4])
    copy_up = pltpu.make_async_copy(up_hbm, up, sems.at[5])
    copies = []
    for g in range(4):
        rows = slice(GROUP * g, GROUP * (g + 1))
        copies.append(pltpu.make_async_copy(codes_hbm.at[rows], codes.at[rows], sems.at[g]))
    copy_scales.start()
    copy_up.start()
    for copy in copies:
        copy.start()
    row, col = iota2((512, 512), 0), iota2((512, 512), 1)
    apart = jnp.where(row == 4 * (col & 127) + (col >> 7), 1.0, 0.0).astype(BF16)
    copy_scales.wait()
    copy_up.wait()
    for block in range(8):
        lanes = slice(512 * block, 512 * (block + 1))
        s = dot(scales[:, lanes], apart)
        u = dot(up[:, lanes], apart).astype(BF16)
        for k in range(4):
            to = slice(128 * block, 128 * (block + 1))
            scales_apart[k, :, to] = s[:, 128 * k : 128 * (k + 1)]
            up_apart[k, :, to] = u[:, 128 * k : 128 * (k + 1)]
    for g in range(4):
        copies[g].wait()
        rows = slice(GROUP * g, GROUP * (g + 1))
        for k in range(4):
            nibble = ((codes[rows, :] >> (4 * k)) & 15) - 8
            part = nibble.astype(F32) * scales_apart[k, g : g + 1, :]
            weight[k, rows, :] = part.astype(BF16)


def make_weights(codes, scales, up):
    return pl.pallas_call(
        weights_kernel,
        in_specs=[HBM] * 3,
        out_specs=[VMEM] * 2,
        out_shape=[
            pltpu.VMEM((4, F, C), BF16),
            pltpu.VMEM((4, RANK, C), BF16),
        ],
        scratch_shapes=[
            pltpu.VMEM((F, C), jnp.int32),
            pltpu.VMEM((F // GROUP, 4 * C), BF16),
            pltpu.VMEM((RANK, 4 * C), BF16),
            pltpu.VMEM((4, F // GROUP, C), F32),
            DMA((6,)),
        ],
        compiler_params=PARAMS,
        cost_estimate=pl.CostEstimate(flops=20_000_000, bytes_accessed=20_000_000, transcendentals=0),
        name="weights",
    )(*in_hbm(codes, scales, up))


def lanes_in_order(value):
    halves = value.reshape(2, 8, 8, T)
    return jnp.stack([halves[0], halves[1]], axis=1).reshape(GROUP, T)


def lanes_by_device(value):
    value = value.reshape(8, 2, 8, T)
    return jnp.concatenate([value[:, 0], value[:, 1]], axis=0)


def sign_kernel(
    place, activ_hbm, flags_hbm, down_hbm, cot_hbm, keep, give, activ, flags, down_map, cot, sems
):
    pairs = ((activ_hbm, activ), (flags_hbm, flags), (down_hbm, down_map), (cot_hbm, cot))
    copies = [pltpu.make_async_copy(a, b, sems.at[n]) for n, (a, b) in enumerate(pairs)]
    for copy in copies:
        copy.start()
    row, col = iota2((O, O), 0), iota2((O, O), 1)
    apart = jnp.where(col == 4 * (row & 63) + (row >> 6), 1.0, 0.0).astype(BF16)
    eye = iota2((GROUP, GROUP), 0) == iota2((GROUP, GROUP), 1)
    lane, rank = iota2((RANK, 2 * RANK), 1), iota2((RANK, 2 * RANK), 0)
    left = jnp.where(lane == rank, 1.0, 0.0).astype(BF16)
    right = jnp.where(lane == rank + RANK, 1.0, 0.0).astype(BF16)
    for copy in copies:
        copy.wait()
    parts = []
    for h in range(4):
        sign = (2 * flags[h : h + 1, :] - 1).astype(F32)
        diagonal = jnp.where(eye, sign, 0.0).astype(BF16)
        parts.append(dot(diagonal, activ[GROUP * h : GROUP * (h + 1), :]))
    for h in (0, 2):
        even = down_map[:, GROUP * h : GROUP * (h + 1)]
        odd = down_map[:, GROUP * (h + 1) : GROUP * (h + 2)]
        parts.append(dot_00(even, left) + dot_00(odd, right))
    parts = [part.reshape(8, 2, 8, T) for part in parts]
    low, high = (
        jnp.concatenate([part[:, n] for part in parts], axis=1).reshape(384, T) for n in range(2)
    )
    keep[0:384, :] = jnp.where(place[1] == 0, low, high).astype(BF16)
    give[0:384, :] = jnp.where(place[1] == 0, high, low).astype(BF16)
    own = dot(apart, cot[...]).astype(BF16)
    keep[384:640, :] = own
    give[384:640, :] = own


def sign(place, activ, flags, down_t, cot):
    return pl.pallas_call(
        sign_kernel,
        in_specs=[SMEM] + [HBM] * 4,
        out_specs=[VMEM] * 2,
        out_shape=[jax.ShapeDtypeStruct((640, T), BF16)] * 2,
        scratch_shapes=[
            pltpu.VMEM((F, T), BF16),
            pltpu.VMEM((4, GROUP), jnp.int32),
            pltpu.VMEM((RANK, F), BF16),
            pltpu.VMEM((O, T), BF16),
            DMA((4,)),
        ],
        compiler_params=PARAMS,
        cost_estimate=pl.CostEstimate(flops=60_000_000, bytes_accessed=600_000, transcendentals=0),
        name="sign",
    )(place, *in_hbm(activ, flags, down_t, cot))


def pack_kernel(own, other, sent):
    for n, part in enumerate((own, other)):
        cot = part[384:640, :]
        for j in range(8):
            sent[j, 48 * n : 48 * (n + 1), :] = part[48 * j : 48 * (j + 1), :]
            sent[j, 96 + 256 * n : 352 + 256 * n, :] = cot


def pack(own, other):
    return pl.pallas_call(
        pack_kernel,
        in_specs=[VMEM] * 2,
        out_specs=VMEM,
        out_shape=pltpu.VMEM((8, 608, T), BF16),
        compiler_params=PARAMS,
        cost_estimate=pl.CostEstimate(flops=0, bytes_accessed=2_000_000, transcendentals=0),
        name="pack",
    )(own, other)


def turn_kernel(place, got, weight, up_apart, down_hbm, sent, back_out, cot, down_t, sem):
    copy_down = pltpu.make_async_copy(down_hbm, down_t, sem)
    copy_down.start()
    one, two = got[:, 0:48, :].astype(F32), got[:, 48:96, :].astype(F32)
    low = jnp.where(place[1] == 0, one, two)
    high = jnp.where(place[1] == 0, two, one)
    both = jnp.concatenate([low, high], axis=0)
    v = butterfly(both[:, 0:32].reshape(HEADS, 8, T), 6) * 0.125
    sent[:, 0:32, :] = v.reshape(NT, 32, T).astype(BF16)
    pairs = v.reshape(NT, 2, 2, 8, T)
    even = pairs[:, :, 0].reshape(256, T).astype(BF16)
    odd = pairs[:, :, 1].reshape(256, T).astype(BF16)
    maps = both[:, 32:48].reshape(256, 2 * RANK).astype(BF16)
    down = dot_00(maps, even)[0:RANK] + dot_00(maps, odd)[RANK : 2 * RANK]
    down = down.astype(BF16)
    for q in range(NT):
        sent[q, 64:128, :] = down
    for n in range(2):
        start = 512 * (place[1] ^ n)
        for j in range(8):
            rows = pl.ds(pl.multiple_of(start + 64 * j, 64), 64)
            for k in range(4):
                at = 96 + 256 * n + 64 * k
                cot[k, rows, :] = got[j, at : at + 64, :]
    copy_down.wait()
    back = jnp.zeros((RANK, T), F32)
    for k in range(4):
        back = back + dot(up_apart[k], cot[k])
    back_out[...] = back
    high, low = split(back)
    for h in range(4):
        rows = slice(GROUP * h, GROUP * (h + 1))
        maps = down_t[:, rows]
        g = ADAPTER_SCALE * (dot_00(maps, high) + dot_00(maps, low))
        for k in range(4):
            g = g + dot(weight[k, rows, :], cot[k])
        g = lanes_by_device(g)
        if h % 2 == 0:
            first = g
        else:
            both = jnp.concatenate([first, g], axis=1)
            sent[:, 24 + 8 * h : 40 + 8 * h, :] = both.astype(BF16)


def turn(place, got, weight, up_apart, down_t):
    return pl.pallas_call(
        turn_kernel,
        in_specs=[SMEM] + [VMEM] * 3 + [HBM],
        out_specs=[VMEM] * 2,
        out_shape=[
            jax.ShapeDtypeStruct((NT, 128, T), BF16),
            jax.ShapeDtypeStruct((RANK, T), F32),
        ],
        scratch_shapes=[
            pltpu.VMEM((4, C, T), BF16),
            pltpu.VMEM((RANK, F), BF16),
            DMA(()),
        ],
        compiler_params=PARAMS,
        cost_estimate=pl.CostEstimate(flops=600_000_000, bytes_accessed=7_000_000, transcendentals=0),
        name="turn",
    )(place, got, *in_vmem(weight, up_apart), *in_hbm(down_t))


def adapter_kernel(got, mixed, back, cot, down, sums):
    total = jnp.sum(got[:, 64:128, :].astype(F32), axis=0)
    down[...] = total
    high, low = split(total)
    back_high, back_low = split(back[...])
    for h in range(4):
        rows = slice(GROUP * h, GROUP * (h + 1))
        product = dot_11(back_high, mixed[rows, :]) + dot_11(back_low, mixed[rows, :])
        sums[RANK * h : RANK * (h + 1), :] = product
    for half in range(2):
        c = cot[GROUP * half : GROUP * (half + 1), :]
        sums[256 + RANK * half : 320 + RANK * half, :] = dot_11(high, c) + dot_11(low, c)


def adapter(got, mixed, back, cot):
    return pl.pallas_call(
        adapter_kernel,
        in_specs=[VMEM] * 4,
        out_specs=[VMEM] * 2,
        out_shape=[
            jax.ShapeDtypeStruct((RANK, T), F32),
            jax.ShapeDtypeStruct((384, T), F32),
        ],
        compiler_params=PARAMS,
        cost_estimate=pl.CostEstimate(flops=30_000_000, bytes_accessed=1_000_000, transcendentals=0),
        name="adapter",
    )(got, mixed, back, cot)


def project_kernel(got, weight, sent, mixed):
    v = got[:, 0:32, :].astype(F32).reshape(NT, 4, 8, T)
    for h in range(4):
        mixed[GROUP * h : GROUP * (h + 1), :] = lanes_in_order(v[:, h]).astype(BF16)
    g = got[:, 32:64, :].astype(F32).reshape(HEADS, 8, T)
    g = butterfly(g, 6) * 0.125
    sent[:, 256:288, :] = g.reshape(NT, 32, T).astype(BF16)
    for k in range(4):
        share = dot_00(weight[k], mixed[...])
        sent[:, 64 * k : 64 * (k + 1), :] = share.reshape(NT, 64, T).astype(BF16)


def project(got, weight):
    return pl.pallas_call(
        project_kernel,
        in_specs=[VMEM] * 2,
        out_specs=[VMEM] * 2,
        out_shape=[
            jax.ShapeDtypeStruct((NT, 288, T), BF16),
            jax.ShapeDtypeStruct((F, T), BF16),
        ],
        compiler_params=PARAMS,
        cost_estimate=pl.CostEstimate(flops=540_000_000, bytes_accessed=6_000_000, transcendentals=0),
        name="project",
    )(got, *in_vmem(weight))


def finish_kernel(place, got, up, down, flags, out, input_gradient, own, sem):
    lanes = pl.ds(pl.multiple_of(place[0] * O, O), O)
    copy = pltpu.make_async_copy(up.at[:, lanes], own, sem)
    copy.start()
    total = jnp.sum(got[:, 0:256, :].astype(F32), axis=0)
    row, col = iota2((O, O), 0), iota2((O, O), 1)
    together = jnp.where(row == 4 * (col & 63) + (col >> 6), 1.0, 0.0).astype(BF16)
    high, low = split(total)
    down_high, down_low = split(down[...])
    copy.wait()
    adapter = dot_00(own[...], down_high) + dot_00(own[...], down_low)
    out[...] = (dot(together, high) + dot(together, low) + ADAPTER_SCALE * adapter).astype(BF16)
    eye = iota2((GROUP, GROUP), 0) == iota2((GROUP, GROUP), 1)
    g = got[:, 256:288, :].astype(F32).reshape(NT, 4, 8, T)
    for h in range(4):
        sign = (2 * flags[h : h + 1, :] - 1).astype(F32)
        diagonal = jnp.where(eye, sign, 0.0).astype(BF16)
        part = lanes_in_order(g[:, h]).astype(BF16)
        input_gradient[GROUP * h : GROUP * (h + 1), :] = dot(diagonal, part).astype(BF16)


def finish(place, got, up, down, flags):
    return pl.pallas_call(
        finish_kernel,
        in_specs=[SMEM, VMEM, HBM, VMEM, VMEM],
        out_specs=[VMEM] * 2,
        out_shape=[
            jax.ShapeDtypeStruct((O, T), BF16),
            jax.ShapeDtypeStruct((F, T), BF16),
        ],
        scratch_shapes=[pltpu.VMEM((RANK, O), BF16), DMA(())],
        compiler_params=PARAMS,
        cost_estimate=pl.CostEstimate(flops=40_000_000, bytes_accessed=1_700_000, transcendentals=0),
        name="finish",
    )(place, got, *in_hbm(up), down, flags)


def gradients_kernel(sums, down_gradient, up_gradient):
    multiplier = ADAPTER_SCALE / 64.0
    for h in range(4):
        lanes = slice(GROUP * h, GROUP * (h + 1))
        down_gradient[:, lanes] = sums[RANK * h : RANK * (h + 1), :] * multiplier
    for half in range(2):
        lanes = slice(GROUP * half, GROUP * (half + 1))
        up_gradient[:, lanes] = sums[256 + RANK * half : 320 + RANK * half, :] * multiplier


def gradients(sums):
    return pl.pallas_call(
        gradients_kernel,
        in_specs=[VMEM],
        out_specs=[VMEM, VMEM],
        out_shape=[
            jax.ShapeDtypeStruct((RANK, F), F32),
            jax.ShapeDtypeStruct((RANK, O), F32),
        ],
        compiler_params=PARAMS,
        cost_estimate=pl.CostEstimate(flops=100_000, bytes_accessed=500_000, transcendentals=0),
        name="gradients",
    )(sums)


def exchange(value):
    return lax.all_to_all(value, "tensor", 0, 0, tiled=True)


def gather(value, masks):
    groups = {}
    for device in range(lax.axis_size("dp")):
        members = [device]
        for mask in masks:
            members += [member ^ mask for member in members]
        groups[min(members)] = sorted(members)
    return lax.all_gather(value, "dp", axis=0, axis_index_groups=list(groups.values()))


def sum_over(value, masks):
    terms = gather(value.astype(BF16), masks)
    terms = [terms[n].astype(F32) for n in range(terms.shape[0])]
    while len(terms) > 1:
        terms = [terms[n] + terms[n + 1] for n in range(0, len(terms), 2)]
    return terms[0]


def local(activ, flags, codes, scales, down_map, up, cot):
    replica = lax.axis_index("dp")
    me = lax.axis_index("tensor")
    place = jnp.stack([me, me >> 3]).astype(jnp.int32)
    flags = flags.reshape(4, GROUP)
    down_t = down_map.T
    own, give = sign(place, activ, flags, down_t, cot)
    other = lax.ppermute(give, "tensor", [(source, source ^ 8) for source in range(NT)])
    weight, up_apart = make_weights(codes, scales, up)
    other, weight = lax.optimization_barrier((other, weight))
    halves = [list(range(8)), list(range(8, NT))]
    got = lax.all_to_all(
        pack(own, other), "tensor", 0, 0, tiled=True, axis_index_groups=halves
    )
    sent, back = turn(place, got, weight, up_apart, down_t)
    got = exchange(sent)
    sent, mixed = project(got, weight)
    down, sums = adapter(got, mixed, back, cot)
    got = exchange(sent)
    half = lax.dynamic_slice_in_dim(sum_over(sums, (1, 2)), 192 * (replica & 1), 192)
    half = sum_over(half, (4,))
    half = sum_over(half, (12,)).astype(BF16)
    pairs = [(source, source ^ 16) for source in range(lax.axis_size("dp"))]
    other = lax.ppermute(half, "dp", pairs)
    out, input_gradient = finish(place, got, up, down, flags)
    other, out, input_gradient = lax.optimization_barrier((other, out, input_gradient))
    half = half.astype(F32) + other.astype(F32)
    down_gradient, up_gradient = gradients(gather(half, (1,)).reshape(384, T))
    return out, input_gradient, down_gradient.T, up_gradient


def solution(mesh):
    in_specs = (
        P("tensor", "dp"),
        P("tensor"),
        P("tensor", None),
        P("tensor", None),
        P("tensor", None),
        P(),
        P("tensor", "dp"),
    )
    out_specs = (P("tensor", "dp"), P("tensor", "dp"), P("tensor", None), P(None, "tensor"))
    return jax.shard_map(local, mesh=mesh, in_specs=in_specs, out_specs=out_specs, check_vma=False)
```

```python
import jax
import jax.numpy as jnp
from jax import lax
from jax.experimental import pallas as pl
from jax.experimental.pallas import tpu as pltpu
from jax.sharding import PartitionSpec as P

HEADS = 64
GROUP = 128
RANK = 64
NT = 16
F = 512
O = 256
C = 1024
T = 128
ADAPTER_SCALE = 0.5
F32 = jnp.float32
BF16 = jnp.bfloat16
PARAMS = pltpu.CompilerParams(vmem_limit_bytes=24 * 1024 * 1024)
VMEM = pl.BlockSpec(memory_space=pltpu.VMEM)
SMEM = pl.BlockSpec(memory_space=pltpu.SMEM)
HBM = pl.BlockSpec(memory_space=pltpu.HBM)
DMA = pltpu.SemaphoreType.DMA


def in_hbm(*arrays):
    return [pltpu.with_memory_space_constraint(a, pltpu.HBM) for a in arrays]


def in_vmem(*arrays):
    return [pltpu.with_memory_space_constraint(a, pltpu.VMEM) for a in arrays]


def dot(a, b):
    return jnp.dot(a, b, preferred_element_type=F32)


def dot_00(a, b):
    return lax.dot_general(a, b, (((0,), (0,)), ((), ())), preferred_element_type=F32)


def dot_11(a, b):
    return lax.dot_general(a, b, (((1,), (1,)), ((), ())), preferred_element_type=F32)


def split(a):
    high = a.astype(BF16)
    return high, (a - high.astype(F32)).astype(BF16)


def butterfly(v, bits):
    n = v.shape[0]
    rest = v.shape[1:]
    for bit in range(bits):
        w = v.reshape((n >> (bit + 1), 2, 1 << bit) + rest)
        low, high = w[:, 0], w[:, 1]
        v = jnp.stack([low + high, low - high], axis=1).reshape((n,) + rest)
    return v


def iota2(shape, dim):
    return lax.broadcasted_iota(jnp.int32, shape, dim)


def weights_kernel(
    codes_hbm, scales_hbm, up_hbm, weight, up_apart,
    codes, scales, up, scales_apart, sems,
):
    copy_scales = pltpu.make_async_copy(scales_hbm, scales, sems.at[4])
    copy_up = pltpu.make_async_copy(up_hbm, up, sems.at[5])
    copies = []
    for g in range(4):
        rows = slice(GROUP * g, GROUP * (g + 1))
        copies.append(pltpu.make_async_copy(codes_hbm.at[rows], codes.at[rows], sems.at[g]))
    copy_scales.start()
    copy_up.start()
    for copy in copies:
        copy.start()
    row, col = iota2((512, 512), 0), iota2((512, 512), 1)
    apart = jnp.where(row == 4 * (col & 127) + (col >> 7), 1.0, 0.0).astype(BF16)
    copy_scales.wait()
    copy_up.wait()
    for block in range(8):
        lanes = slice(512 * block, 512 * (block + 1))
        s = dot(scales[:, lanes], apart)
        u = dot(up[:, lanes], apart).astype(BF16)
        for k in range(4):
            to = slice(128 * block, 128 * (block + 1))
            scales_apart[k, :, to] = s[:, 128 * k : 128 * (k + 1)]
            up_apart[k, :, to] = u[:, 128 * k : 128 * (k + 1)]
    for g in range(4):
        copies[g].wait()
        rows = slice(GROUP * g, GROUP * (g + 1))
        for k in range(4):
            nibble = ((codes[rows, :] >> (4 * k)) & 15) - 8
            part = nibble.astype(F32) * scales_apart[k, g : g + 1, :]
            weight[k, rows, :] = part.astype(BF16)


def make_weights(codes, scales, up):
    return pl.pallas_call(
        weights_kernel,
        in_specs=[HBM] * 3,
        out_specs=[VMEM] * 2,
        out_shape=[
            pltpu.VMEM((4, F, C), BF16),
            pltpu.VMEM((4, RANK, C), BF16),
        ],
        scratch_shapes=[
            pltpu.VMEM((F, C), jnp.int32),
            pltpu.VMEM((F // GROUP, 4 * C), BF16),
            pltpu.VMEM((RANK, 4 * C), BF16),
            pltpu.VMEM((4, F // GROUP, C), F32),
            DMA((6,)),
        ],
        compiler_params=PARAMS,
        cost_estimate=pl.CostEstimate(flops=20_000_000, bytes_accessed=20_000_000, transcendentals=0),
        name="weights",
    )(*in_hbm(codes, scales, up))


def lanes_in_order(value):
    halves = value.reshape(2, 8, 8, T)
    return jnp.stack([halves[0], halves[1]], axis=1).reshape(GROUP, T)


def lanes_by_device(value):
    value = value.reshape(8, 2, 8, T)
    return jnp.concatenate([value[:, 0], value[:, 1]], axis=0)


def sign_kernel(
    place, activ_hbm, flags_hbm, down_hbm, cot_hbm, keep, give, activ, flags, down_map, cot, sems
):
    pairs = ((activ_hbm, activ), (flags_hbm, flags), (down_hbm, down_map), (cot_hbm, cot))
    copies = [pltpu.make_async_copy(a, b, sems.at[n]) for n, (a, b) in enumerate(pairs)]
    for copy in copies:
        copy.start()
    row, col = iota2((O, O), 0), iota2((O, O), 1)
    apart = jnp.where(col == 4 * (row & 63) + (row >> 6), 1.0, 0.0).astype(BF16)
    eye = iota2((GROUP, GROUP), 0) == iota2((GROUP, GROUP), 1)
    lane, rank = iota2((RANK, 2 * RANK), 1), iota2((RANK, 2 * RANK), 0)
    left = jnp.where(lane == rank, 1.0, 0.0).astype(BF16)
    right = jnp.where(lane == rank + RANK, 1.0, 0.0).astype(BF16)
    for copy in copies:
        copy.wait()
    parts = []
    for h in range(4):
        sign = (2 * flags[h : h + 1, :] - 1).astype(F32)
        diagonal = jnp.where(eye, sign, 0.0).astype(BF16)
        parts.append(dot(diagonal, activ[GROUP * h : GROUP * (h + 1), :]))
    for h in (0, 2):
        even = down_map[:, GROUP * h : GROUP * (h + 1)]
        odd = down_map[:, GROUP * (h + 1) : GROUP * (h + 2)]
        parts.append(dot_00(even, left) + dot_00(odd, right))
    parts = [part.reshape(8, 2, 8, T) for part in parts]
    low, high = (
        jnp.concatenate([part[:, n] for part in parts], axis=1).reshape(384, T) for n in range(2)
    )
    keep[0:384, :] = jnp.where(place[0] < 8, low, high).astype(BF16)
    give[0:384, :] = jnp.where(place[0] < 8, high, low).astype(BF16)
    own = dot(apart, cot[...]).astype(BF16)
    keep[384:640, :] = own
    give[384:640, :] = own


def sign(place, activ, flags, down_t, cot):
    return pl.pallas_call(
        sign_kernel,
        in_specs=[SMEM] + [HBM] * 4,
        out_specs=[VMEM] * 2,
        out_shape=[jax.ShapeDtypeStruct((640, T), BF16)] * 2,
        scratch_shapes=[
            pltpu.VMEM((F, T), BF16),
            pltpu.VMEM((4, GROUP), jnp.int32),
            pltpu.VMEM((RANK, F), BF16),
            pltpu.VMEM((O, T), BF16),
            DMA((4,)),
        ],
        compiler_params=PARAMS,
        cost_estimate=pl.CostEstimate(flops=60_000_000, bytes_accessed=600_000, transcendentals=0),
        name="sign",
    )(place, *in_hbm(activ, flags, down_t, cot))


def pack_kernel(own, other, sent):
    for n, part in enumerate((own, other)):
        cot = part[384:640, :]
        for j in range(8):
            sent[j, 48 * n : 48 * (n + 1), :] = part[48 * j : 48 * (j + 1), :]
            sent[j, 96 + 256 * n : 352 + 256 * n, :] = cot


def pack(own, other):
    return pl.pallas_call(
        pack_kernel,
        in_specs=[VMEM] * 2,
        out_specs=VMEM,
        out_shape=pltpu.VMEM((8, 608, T), BF16),
        compiler_params=PARAMS,
        cost_estimate=pl.CostEstimate(flops=0, bytes_accessed=2_000_000, transcendentals=0),
        name="pack",
    )(own, other)


def turn_kernel(place, got, weight, up_apart, down_hbm, sent, back_out, cot, down_t, sem):
    copy_down = pltpu.make_async_copy(down_hbm, down_t, sem)
    copy_down.start()
    one, two = got[:, 0:48, :].astype(F32), got[:, 48:96, :].astype(F32)
    low = jnp.where(place[0] < 8, one, two)
    high = jnp.where(place[0] < 8, two, one)
    both = jnp.concatenate([low, high], axis=0)
    v = butterfly(both[:, 0:32].reshape(HEADS, 8, T), 6) * 0.125
    sent[:, 0:32, :] = v.reshape(NT, 32, T).astype(BF16)
    pairs = v.reshape(NT, 2, 2, 8, T)
    even = pairs[:, :, 0].reshape(256, T).astype(BF16)
    odd = pairs[:, :, 1].reshape(256, T).astype(BF16)
    maps = both[:, 32:48].reshape(256, 2 * RANK).astype(BF16)
    down = dot_00(maps, even)[0:RANK] + dot_00(maps, odd)[RANK : 2 * RANK]
    down = down.astype(BF16)
    for q in range(NT):
        sent[q, 64:128, :] = down
    for n in range(2):
        start = 512 * ((place[0] >> 3) ^ n)
        for j in range(8):
            rows = pl.ds(pl.multiple_of(start + 64 * j, 64), 64)
            for k in range(4):
                at = 96 + 256 * n + 64 * k
                cot[k, rows, :] = got[j, at : at + 64, :]
    copy_down.wait()
    back = jnp.zeros((RANK, T), F32)
    for k in range(4):
        back = back + dot(up_apart[k], cot[k])
    back_out[...] = back
    high, low = split(back)
    for h in range(4):
        rows = slice(GROUP * h, GROUP * (h + 1))
        maps = down_t[:, rows]
        g = ADAPTER_SCALE * (dot_00(maps, high) + dot_00(maps, low))
        for k in range(4):
            g = g + dot(weight[k, rows, :], cot[k])
        g = lanes_by_device(g)
        if h % 2 == 0:
            first = g
        else:
            both = jnp.concatenate([first, g], axis=1)
            sent[:, 24 + 8 * h : 40 + 8 * h, :] = both.astype(BF16)


def turn(place, got, weight, up_apart, down_t):
    return pl.pallas_call(
        turn_kernel,
        in_specs=[SMEM] + [VMEM] * 3 + [HBM],
        out_specs=[VMEM] * 2,
        out_shape=[
            jax.ShapeDtypeStruct((NT, 128, T), BF16),
            jax.ShapeDtypeStruct((RANK, T), F32),
        ],
        scratch_shapes=[
            pltpu.VMEM((4, C, T), BF16),
            pltpu.VMEM((RANK, F), BF16),
            DMA(()),
        ],
        compiler_params=PARAMS,
        cost_estimate=pl.CostEstimate(flops=600_000_000, bytes_accessed=7_000_000, transcendentals=0),
        name="turn",
    )(place, got, *in_vmem(weight, up_apart), *in_hbm(down_t))


def adapter_kernel(got, mixed, back, cot, down, sums):
    total = jnp.sum(got[:, 64:128, :].astype(F32), axis=0)
    down[...] = total
    high, low = split(total)
    back_high, back_low = split(back[...])
    for h in range(4):
        rows = slice(GROUP * h, GROUP * (h + 1))
        product = dot_11(back_high, mixed[rows, :]) + dot_11(back_low, mixed[rows, :])
        sums[RANK * h : RANK * (h + 1), :] = product
    for half in range(2):
        c = cot[GROUP * half : GROUP * (half + 1), :]
        sums[256 + RANK * half : 320 + RANK * half, :] = dot_11(high, c) + dot_11(low, c)


def adapter(got, mixed, back, cot):
    return pl.pallas_call(
        adapter_kernel,
        in_specs=[VMEM] * 4,
        out_specs=[VMEM] * 2,
        out_shape=[
            jax.ShapeDtypeStruct((RANK, T), F32),
            jax.ShapeDtypeStruct((384, T), F32),
        ],
        compiler_params=PARAMS,
        cost_estimate=pl.CostEstimate(flops=30_000_000, bytes_accessed=1_000_000, transcendentals=0),
        name="adapter",
    )(got, mixed, back, cot)


def project_kernel(got, weight, sent, mixed):
    v = got[:, 0:32, :].astype(F32).reshape(NT, 4, 8, T)
    for h in range(4):
        mixed[GROUP * h : GROUP * (h + 1), :] = lanes_in_order(v[:, h]).astype(BF16)
    g = got[:, 32:64, :].astype(F32).reshape(HEADS, 8, T)
    g = butterfly(g, 6) * 0.125
    sent[:, 256:288, :] = g.reshape(NT, 32, T).astype(BF16)
    for k in range(4):
        share = dot_00(weight[k], mixed[...])
        sent[:, 64 * k : 64 * (k + 1), :] = share.reshape(NT, 64, T).astype(BF16)


def project(got, weight):
    return pl.pallas_call(
        project_kernel,
        in_specs=[VMEM] * 2,
        out_specs=[VMEM] * 2,
        out_shape=[
            jax.ShapeDtypeStruct((NT, 288, T), BF16),
            jax.ShapeDtypeStruct((F, T), BF16),
        ],
        compiler_params=PARAMS,
        cost_estimate=pl.CostEstimate(flops=540_000_000, bytes_accessed=6_000_000, transcendentals=0),
        name="project",
    )(got, *in_vmem(weight))


def finish_kernel(place, got, up, down, flags, out, input_gradient, own, sem):
    lanes = pl.ds(pl.multiple_of(place[0] * O, O), O)
    copy = pltpu.make_async_copy(up.at[:, lanes], own, sem)
    copy.start()
    total = jnp.sum(got[:, 0:256, :].astype(F32), axis=0)
    row, col = iota2((O, O), 0), iota2((O, O), 1)
    together = jnp.where(row == 4 * (col & 63) + (col >> 6), 1.0, 0.0).astype(BF16)
    high, low = split(total)
    down_high, down_low = split(down[...])
    copy.wait()
    adapter = dot_00(own[...], down_high) + dot_00(own[...], down_low)
    out[...] = (dot(together, high) + dot(together, low) + ADAPTER_SCALE * adapter).astype(BF16)
    eye = iota2((GROUP, GROUP), 0) == iota2((GROUP, GROUP), 1)
    g = got[:, 256:288, :].astype(F32).reshape(NT, 4, 8, T)
    for h in range(4):
        sign = (2 * flags[h : h + 1, :] - 1).astype(F32)
        diagonal = jnp.where(eye, sign, 0.0).astype(BF16)
        part = lanes_in_order(g[:, h]).astype(BF16)
        input_gradient[GROUP * h : GROUP * (h + 1), :] = dot(diagonal, part).astype(BF16)


def finish(place, got, up, down, flags):
    return pl.pallas_call(
        finish_kernel,
        in_specs=[SMEM, VMEM, HBM, VMEM, VMEM],
        out_specs=[VMEM] * 2,
        out_shape=[
            jax.ShapeDtypeStruct((O, T), BF16),
            jax.ShapeDtypeStruct((F, T), BF16),
        ],
        scratch_shapes=[pltpu.VMEM((RANK, O), BF16), DMA(())],
        compiler_params=PARAMS,
        cost_estimate=pl.CostEstimate(flops=40_000_000, bytes_accessed=1_700_000, transcendentals=0),
        name="finish",
    )(place, got, *in_hbm(up), down, flags)


def gradients_kernel(sums, down_gradient, up_gradient):
    multiplier = ADAPTER_SCALE / 64.0
    for h in range(4):
        lanes = slice(GROUP * h, GROUP * (h + 1))
        down_gradient[:, lanes] = sums[RANK * h : RANK * (h + 1), :] * multiplier
    for half in range(2):
        lanes = slice(GROUP * half, GROUP * (half + 1))
        up_gradient[:, lanes] = sums[256 + RANK * half : 320 + RANK * half, :] * multiplier


def gradients(sums):
    return pl.pallas_call(
        gradients_kernel,
        in_specs=[VMEM],
        out_specs=[VMEM, VMEM],
        out_shape=[
            jax.ShapeDtypeStruct((RANK, F), F32),
            jax.ShapeDtypeStruct((RANK, O), F32),
        ],
        compiler_params=PARAMS,
        cost_estimate=pl.CostEstimate(flops=100_000, bytes_accessed=500_000, transcendentals=0),
        name="gradients",
    )(sums)


def exchange(value):
    return lax.all_to_all(value, "tensor", 0, 0, tiled=True)


def gather(value, masks):
    groups = {}
    for device in range(lax.axis_size("dp")):
        members = [device]
        for mask in masks:
            members += [member ^ mask for member in members]
        groups[min(members)] = sorted(members)
    return lax.all_gather(value, "dp", axis=0, axis_index_groups=list(groups.values()))


def sum_over(value, masks):
    terms = gather(value.astype(BF16), masks)
    terms = [terms[n].astype(F32) for n in range(terms.shape[0])]
    while len(terms) > 1:
        terms = [terms[n] + terms[n + 1] for n in range(0, len(terms), 2)]
    return terms[0]


def local(activ, flags, codes, scales, down_map, up, cot):
    replica = lax.axis_index("dp")
    me = lax.axis_index("tensor")
    place = me.reshape(1)
    flags = flags.reshape(4, GROUP)
    down_t = down_map.T
    own, give = sign(place, activ, flags, down_t, cot)
    other = lax.ppermute(give, "tensor", [(source, source ^ 8) for source in range(NT)])
    weight, up_apart = make_weights(codes, scales, up)
    other, weight = lax.optimization_barrier((other, weight))
    halves = [list(range(8)), list(range(8, NT))]
    got = lax.all_to_all(
        pack(own, other), "tensor", 0, 0, tiled=True, axis_index_groups=halves
    )
    sent, back = turn(place, got, weight, up_apart, down_t)
    got = exchange(sent)
    sent, mixed = project(got, weight)
    down, sums = adapter(got, mixed, back, cot)
    got = exchange(sent)
    half = lax.dynamic_slice_in_dim(sum_over(sums, (1, 2)), 192 * (replica & 1), 192)
    half = sum_over(half, (4,))
    half = sum_over(half, (12,)).astype(BF16)
    pairs = [(source, source ^ 16) for source in range(lax.axis_size("dp"))]
    other = lax.ppermute(half, "dp", pairs)
    out, input_gradient = finish(place, got, up, down, flags)
    other, out, input_gradient = lax.optimization_barrier((other, out, input_gradient))
    half = half.astype(F32) + other.astype(F32)
    down_gradient, up_gradient = gradients(gather(half, (1,)).reshape(384, T))
    return out, input_gradient, down_gradient.T, up_gradient


def solution(mesh):
    in_specs = (
        P("tensor", "dp"),
        P("tensor"),
        P("tensor", None),
        P("tensor", None),
        P("tensor", None),
        P(),
        P("tensor", "dp"),
    )
    out_specs = (P("tensor", "dp"), P("tensor", "dp"), P("tensor", None), P(None, "tensor"))
    return jax.shard_map(local, mesh=mesh, in_specs=in_specs, out_specs=out_specs, check_vma=False)
```

```python
import jax
import jax.numpy as jnp
from jax import lax
from jax.experimental import pallas as pl
from jax.experimental.pallas import tpu as pltpu
from jax.sharding import PartitionSpec as P

HEADS = 64
GROUP = 128
RANK = 64
NT = 16
F = 512
O = 256
C = 1024
T = 128
ADAPTER_SCALE = 0.5
F32 = jnp.float32
BF16 = jnp.bfloat16
PARAMS = pltpu.CompilerParams(vmem_limit_bytes=24 * 1024 * 1024)
VMEM = pl.BlockSpec(memory_space=pltpu.VMEM)
SMEM = pl.BlockSpec(memory_space=pltpu.SMEM)
HBM = pl.BlockSpec(memory_space=pltpu.HBM)
DMA = pltpu.SemaphoreType.DMA


def in_hbm(*arrays):
    return [pltpu.with_memory_space_constraint(a, pltpu.HBM) for a in arrays]


def in_vmem(*arrays):
    return [pltpu.with_memory_space_constraint(a, pltpu.VMEM) for a in arrays]


def dot(a, b):
    return jnp.dot(a, b, preferred_element_type=F32)


def dot_00(a, b):
    return lax.dot_general(a, b, (((0,), (0,)), ((), ())), preferred_element_type=F32)


def dot_11(a, b):
    return lax.dot_general(a, b, (((1,), (1,)), ((), ())), preferred_element_type=F32)


def split(a):
    high = a.astype(BF16)
    return high, (a - high.astype(F32)).astype(BF16)


def butterfly(v, bits):
    n = v.shape[0]
    rest = v.shape[1:]
    for bit in range(bits):
        w = v.reshape((n >> (bit + 1), 2, 1 << bit) + rest)
        low, high = w[:, 0], w[:, 1]
        v = jnp.stack([low + high, low - high], axis=1).reshape((n,) + rest)
    return v


def iota2(shape, dim):
    return lax.broadcasted_iota(jnp.int32, shape, dim)


def weights_kernel(
    codes_hbm, scales_hbm, up_hbm, weight, weight_t, up_apart,
    codes, scales, up, scales_apart, sems,
):
    copy_scales = pltpu.make_async_copy(scales_hbm, scales, sems.at[4])
    copy_up = pltpu.make_async_copy(up_hbm, up, sems.at[5])
    copies = []
    for g in range(4):
        rows = slice(GROUP * g, GROUP * (g + 1))
        copies.append(pltpu.make_async_copy(codes_hbm.at[rows], codes.at[rows], sems.at[g]))
    copy_scales.start()
    copy_up.start()
    for copy in copies:
        copy.start()
    row, col = iota2((512, 512), 0), iota2((512, 512), 1)
    apart = jnp.where(row == 4 * (col & 127) + (col >> 7), 1.0, 0.0).astype(BF16)
    copy_scales.wait()
    copy_up.wait()
    for block in range(8):
        lanes = slice(512 * block, 512 * (block + 1))
        s = dot(scales[:, lanes], apart)
        u = dot(up[:, lanes], apart).astype(BF16)
        for k in range(4):
            to = slice(128 * block, 128 * (block + 1))
            scales_apart[k, :, to] = s[:, 128 * k : 128 * (k + 1)]
            up_apart[k, :, to] = u[:, 128 * k : 128 * (k + 1)]
    for g in range(4):
        copies[g].wait()
        rows = slice(GROUP * g, GROUP * (g + 1))
        for k in range(4):
            nibble = ((codes[rows, :] >> (4 * k)) & 15) - 8
            part = nibble.astype(F32) * scales_apart[k, g : g + 1, :]
            weight[k, rows, :] = part.astype(BF16)
            weight_t[k, :, rows] = part.T.astype(BF16)


def make_weights(codes, scales, up):
    return pl.pallas_call(
        weights_kernel,
        in_specs=[HBM] * 3,
        out_specs=[VMEM] * 3,
        out_shape=[
            pltpu.VMEM((4, F, C), BF16),
            pltpu.VMEM((4, C, F), BF16),
            pltpu.VMEM((4, RANK, C), BF16),
        ],
        scratch_shapes=[
            pltpu.VMEM((F, C), jnp.int32),
            pltpu.VMEM((F // GROUP, 4 * C), BF16),
            pltpu.VMEM((RANK, 4 * C), BF16),
            pltpu.VMEM((4, F // GROUP, C), F32),
            DMA((6,)),
        ],
        compiler_params=PARAMS,
        cost_estimate=pl.CostEstimate(flops=20_000_000, bytes_accessed=20_000_000, transcendentals=0),
        name="weights",
    )(*in_hbm(codes, scales, up))


def lanes_in_order(value):
    halves = value.reshape(2, 8, 8, T)
    return jnp.stack([halves[0], halves[1]], axis=1).reshape(GROUP, T)


def lanes_by_device(value):
    value = value.reshape(8, 2, 8, T)
    return jnp.concatenate([value[:, 0], value[:, 1]], axis=0)


def sign_kernel(
    place, activ_hbm, flags_hbm, down_hbm, cot_hbm, keep, give, activ, flags, down_map, cot, sems
):
    pairs = ((activ_hbm, activ), (flags_hbm, flags), (down_hbm, down_map), (cot_hbm, cot))
    copies = [pltpu.make_async_copy(a, b, sems.at[n]) for n, (a, b) in enumerate(pairs)]
    for copy in copies:
        copy.start()
    row, col = iota2((O, O), 0), iota2((O, O), 1)
    apart = jnp.where(col == 4 * (row & 63) + (row >> 6), 1.0, 0.0).astype(BF16)
    eye = iota2((GROUP, GROUP), 0) == iota2((GROUP, GROUP), 1)
    lane, rank = iota2((RANK, 2 * RANK), 1), iota2((RANK, 2 * RANK), 0)
    left = jnp.where(lane == rank, 1.0, 0.0).astype(BF16)
    right = jnp.where(lane == rank + RANK, 1.0, 0.0).astype(BF16)
    for copy in copies:
        copy.wait()
    parts = []
    for h in range(4):
        sign = (2 * flags[h : h + 1, :] - 1).astype(F32)
        diagonal = jnp.where(eye, sign, 0.0).astype(BF16)
        parts.append(dot(diagonal, activ[GROUP * h : GROUP * (h + 1), :]))
    for h in (0, 2):
        even = down_map[:, GROUP * h : GROUP * (h + 1)]
        odd = down_map[:, GROUP * (h + 1) : GROUP * (h + 2)]
        parts.append(dot_00(even, left) + dot_00(odd, right))
    parts = [part.reshape(8, 2, 8, T) for part in parts]
    low, high = (
        jnp.concatenate([part[:, n] for part in parts], axis=1).reshape(384, T) for n in range(2)
    )
    keep[0:384, :] = jnp.where(place[0] < 8, low, high).astype(BF16)
    give[0:384, :] = jnp.where(place[0] < 8, high, low).astype(BF16)
    own = dot(apart, cot[...]).astype(BF16)
    keep[384:640, :] = own
    give[384:640, :] = own


def sign(place, activ, flags, down_t, cot):
    return pl.pallas_call(
        sign_kernel,
        in_specs=[SMEM] + [HBM] * 4,
        out_specs=[VMEM] * 2,
        out_shape=[jax.ShapeDtypeStruct((640, T), BF16)] * 2,
        scratch_shapes=[
            pltpu.VMEM((F, T), BF16),
            pltpu.VMEM((4, GROUP), jnp.int32),
            pltpu.VMEM((RANK, F), BF16),
            pltpu.VMEM((O, T), BF16),
            DMA((4,)),
        ],
        compiler_params=PARAMS,
        cost_estimate=pl.CostEstimate(flops=60_000_000, bytes_accessed=600_000, transcendentals=0),
        name="sign",
    )(place, *in_hbm(activ, flags, down_t, cot))


def pack_kernel(own, other, sent):
    for n, part in enumerate((own, other)):
        cot = part[384:640, :]
        for j in range(8):
            sent[j, 48 * n : 48 * (n + 1), :] = part[48 * j : 48 * (j + 1), :]
            sent[j, 96 + 256 * n : 352 + 256 * n, :] = cot


def pack(own, other):
    return pl.pallas_call(
        pack_kernel,
        in_specs=[VMEM] * 2,
        out_specs=VMEM,
        out_shape=pltpu.VMEM((8, 608, T), BF16),
        compiler_params=PARAMS,
        cost_estimate=pl.CostEstimate(flops=0, bytes_accessed=2_000_000, transcendentals=0),
        name="pack",
    )(own, other)


def turn_kernel(place, got, weight, up_apart, down_hbm, sent, back_out, cot, down_t, sem):
    copy_down = pltpu.make_async_copy(down_hbm, down_t, sem)
    copy_down.start()
    one, two = got[:, 0:48, :].astype(F32), got[:, 48:96, :].astype(F32)
    low = jnp.where(place[0] < 8, one, two)
    high = jnp.where(place[0] < 8, two, one)
    both = jnp.concatenate([low, high], axis=0)
    v = butterfly(both[:, 0:32].reshape(HEADS, 8, T), 6) * 0.125
    sent[:, 0:32, :] = v.reshape(NT, 32, T).astype(BF16)
    pairs = v.reshape(NT, 2, 2, 8, T)
    even = pairs[:, :, 0].reshape(256, T).astype(BF16)
    odd = pairs[:, :, 1].reshape(256, T).astype(BF16)
    maps = both[:, 32:48].reshape(256, 2 * RANK).astype(BF16)
    down = dot_00(maps, even)[0:RANK] + dot_00(maps, odd)[RANK : 2 * RANK]
    down = down.astype(BF16)
    for q in range(NT):
        sent[q, 64:128, :] = down
    for n in range(2):
        start = 512 * ((place[0] >> 3) ^ n)
        for j in range(8):
            rows = pl.ds(pl.multiple_of(start + 64 * j, 64), 64)
            for k in range(4):
                at = 96 + 256 * n + 64 * k
                cot[k, rows, :] = got[j, at : at + 64, :]
    copy_down.wait()
    back = jnp.zeros((RANK, T), F32)
    for k in range(4):
        back = back + dot(up_apart[k], cot[k])
    back_out[...] = back
    high, low = split(back)
    for h in range(4):
        rows = slice(GROUP * h, GROUP * (h + 1))
        maps = down_t[:, rows]
        g = ADAPTER_SCALE * (dot_00(maps, high) + dot_00(maps, low))
        for k in range(4):
            g = g + dot(weight[k, rows, :], cot[k])
        g = lanes_by_device(g)
        if h % 2 == 0:
            first = g
        else:
            both = jnp.concatenate([first, g], axis=1)
            sent[:, 24 + 8 * h : 40 + 8 * h, :] = both.astype(BF16)


def turn(place, got, weight, up_apart, down_t):
    return pl.pallas_call(
        turn_kernel,
        in_specs=[SMEM] + [VMEM] * 3 + [HBM],
        out_specs=[VMEM] * 2,
        out_shape=[
            jax.ShapeDtypeStruct((NT, 128, T), BF16),
            jax.ShapeDtypeStruct((RANK, T), F32),
        ],
        scratch_shapes=[
            pltpu.VMEM((4, C, T), BF16),
            pltpu.VMEM((RANK, F), BF16),
            DMA(()),
        ],
        compiler_params=PARAMS,
        cost_estimate=pl.CostEstimate(flops=600_000_000, bytes_accessed=7_000_000, transcendentals=0),
        name="turn",
    )(place, got, *in_vmem(weight, up_apart), *in_hbm(down_t))


def adapter_kernel(got, mixed, back, cot, down, sums):
    total = jnp.sum(got[:, 64:128, :].astype(F32), axis=0)
    down[...] = total
    high, low = split(total)
    back_high, back_low = split(back[...])
    for h in range(4):
        rows = slice(GROUP * h, GROUP * (h + 1))
        product = dot_11(back_high, mixed[rows, :]) + dot_11(back_low, mixed[rows, :])
        sums[RANK * h : RANK * (h + 1), :] = product
    for half in range(2):
        c = cot[GROUP * half : GROUP * (half + 1), :]
        sums[256 + RANK * half : 320 + RANK * half, :] = dot_11(high, c) + dot_11(low, c)


def adapter(got, mixed, back, cot):
    return pl.pallas_call(
        adapter_kernel,
        in_specs=[VMEM] * 4,
        out_specs=[VMEM] * 2,
        out_shape=[
            jax.ShapeDtypeStruct((RANK, T), F32),
            jax.ShapeDtypeStruct((384, T), F32),
        ],
        compiler_params=PARAMS,
        cost_estimate=pl.CostEstimate(flops=30_000_000, bytes_accessed=1_000_000, transcendentals=0),
        name="adapter",
    )(got, mixed, back, cot)


def project_kernel(got, weight_t, sent, mixed):
    v = got[:, 0:32, :].astype(F32).reshape(NT, 4, 8, T)
    for h in range(4):
        mixed[GROUP * h : GROUP * (h + 1), :] = lanes_in_order(v[:, h]).astype(BF16)
    g = got[:, 32:64, :].astype(F32).reshape(HEADS, 8, T)
    g = butterfly(g, 6) * 0.125
    sent[:, 256:288, :] = g.reshape(NT, 32, T).astype(BF16)
    for k in range(4):
        share = dot(weight_t[k], mixed[...])
        sent[:, 64 * k : 64 * (k + 1), :] = share.reshape(NT, 64, T).astype(BF16)


def project(got, weight_t):
    return pl.pallas_call(
        project_kernel,
        in_specs=[VMEM] * 2,
        out_specs=[VMEM] * 2,
        out_shape=[
            jax.ShapeDtypeStruct((NT, 288, T), BF16),
            jax.ShapeDtypeStruct((F, T), BF16),
        ],
        compiler_params=PARAMS,
        cost_estimate=pl.CostEstimate(flops=540_000_000, bytes_accessed=6_000_000, transcendentals=0),
        name="project",
    )(got, *in_vmem(weight_t))


def finish_kernel(place, got, up, down, flags, out, input_gradient, own, sem):
    lanes = pl.ds(pl.multiple_of(place[0] * O, O), O)
    copy = pltpu.make_async_copy(up.at[:, lanes], own, sem)
    copy.start()
    total = jnp.sum(got[:, 0:256, :].astype(F32), axis=0)
    row, col = iota2((O, O), 0), iota2((O, O), 1)
    together = jnp.where(row == 4 * (col & 63) + (col >> 6), 1.0, 0.0).astype(BF16)
    high, low = split(total)
    down_high, down_low = split(down[...])
    copy.wait()
    adapter = dot_00(own[...], down_high) + dot_00(own[...], down_low)
    out[...] = (dot(together, high) + dot(together, low) + ADAPTER_SCALE * adapter).astype(BF16)
    eye = iota2((GROUP, GROUP), 0) == iota2((GROUP, GROUP), 1)
    g = got[:, 256:288, :].astype(F32).reshape(NT, 4, 8, T)
    for h in range(4):
        sign = (2 * flags[h : h + 1, :] - 1).astype(F32)
        diagonal = jnp.where(eye, sign, 0.0).astype(BF16)
        part = lanes_in_order(g[:, h]).astype(BF16)
        input_gradient[GROUP * h : GROUP * (h + 1), :] = dot(diagonal, part).astype(BF16)


def finish(place, got, up, down, flags):
    return pl.pallas_call(
        finish_kernel,
        in_specs=[SMEM, VMEM, HBM, VMEM, VMEM],
        out_specs=[VMEM] * 2,
        out_shape=[
            jax.ShapeDtypeStruct((O, T), BF16),
            jax.ShapeDtypeStruct((F, T), BF16),
        ],
        scratch_shapes=[pltpu.VMEM((RANK, O), BF16), DMA(())],
        compiler_params=PARAMS,
        cost_estimate=pl.CostEstimate(flops=40_000_000, bytes_accessed=1_700_000, transcendentals=0),
        name="finish",
    )(place, got, *in_hbm(up), down, flags)


def gradients_kernel(sums, down_gradient, up_gradient):
    multiplier = ADAPTER_SCALE / 64.0
    for h in range(4):
        lanes = slice(GROUP * h, GROUP * (h + 1))
        down_gradient[:, lanes] = sums[RANK * h : RANK * (h + 1), :] * multiplier
    for half in range(2):
        lanes = slice(GROUP * half, GROUP * (half + 1))
        up_gradient[:, lanes] = sums[256 + RANK * half : 320 + RANK * half, :] * multiplier


def gradients(sums):
    return pl.pallas_call(
        gradients_kernel,
        in_specs=[VMEM],
        out_specs=[VMEM, VMEM],
        out_shape=[
            jax.ShapeDtypeStruct((RANK, F), F32),
            jax.ShapeDtypeStruct((RANK, O), F32),
        ],
        compiler_params=PARAMS,
        cost_estimate=pl.CostEstimate(flops=100_000, bytes_accessed=500_000, transcendentals=0),
        name="gradients",
    )(sums)


def exchange(value):
    return lax.all_to_all(value, "tensor", 0, 0, tiled=True)


def gather(value, masks):
    groups = {}
    for device in range(lax.axis_size("dp")):
        members = [device]
        for mask in masks:
            members += [member ^ mask for member in members]
        groups[min(members)] = sorted(members)
    return lax.all_gather(value, "dp", axis=0, axis_index_groups=list(groups.values()))


def sum_over(value, masks):
    terms = gather(value.astype(BF16), masks)
    terms = [terms[n].astype(F32) for n in range(terms.shape[0])]
    while len(terms) > 1:
        terms = [terms[n] + terms[n + 1] for n in range(0, len(terms), 2)]
    return terms[0]


def local(activ, flags, codes, scales, down_map, up, cot):
    replica = lax.axis_index("dp")
    me = lax.axis_index("tensor")
    place = me.reshape(1)
    flags = flags.reshape(4, GROUP)
    down_t = down_map.T
    own, give = sign(place, activ, flags, down_t, cot)
    other = lax.ppermute(give, "tensor", [(source, source ^ 8) for source in range(NT)])
    weight, weight_t, up_apart = make_weights(codes, scales, up)
    other, weight = lax.optimization_barrier((other, weight))
    halves = [list(range(8)), list(range(8, NT))]
    got = lax.all_to_all(
        pack(own, other), "tensor", 0, 0, tiled=True, axis_index_groups=halves
    )
    sent, back = turn(place, got, weight, up_apart, down_t)
    got = exchange(sent)
    sent, mixed = project(got, weight_t)
    down, sums = adapter(got, mixed, back, cot)
    got = exchange(sent)
    half = lax.dynamic_slice_in_dim(sum_over(sums, (1, 2)), 192 * (replica & 1), 192)
    half = sum_over(half, (4,))
    half = sum_over(half, (12,)).astype(BF16)
    pairs = [(source, source ^ 16) for source in range(lax.axis_size("dp"))]
    other = lax.ppermute(half, "dp", pairs)
    out, input_gradient = finish(place, got, up, down, flags)
    other, out, input_gradient = lax.optimization_barrier((other, out, input_gradient))
    half = half.astype(F32) + other.astype(F32)
    down_gradient, up_gradient = gradients(gather(half, (1,)).reshape(384, T))
    return out, input_gradient, down_gradient.T, up_gradient


def solution(mesh):
    in_specs = (
        P("tensor", "dp"),
        P("tensor"),
        P("tensor", None),
        P("tensor", None),
        P("tensor", None),
        P(),
        P("tensor", "dp"),
    )
    out_specs = (P("tensor", "dp"), P("tensor", "dp"), P("tensor", None), P(None, "tensor"))
    return jax.shard_map(local, mesh=mesh, in_specs=in_specs, out_specs=out_specs, check_vma=False)
```
